128 devices in a mesh: feat: 32 (over y, z, core), pair: 4 (over x).
Axes of the slice: x: 4, y: 4, z: 4, core: 2. Of those that a mesh axis runs over, the one named last changes fastest.
Arguments:
- in_factors: bfloat16 [2048, 2, 512, 256], P(('feat', 'pair')), may hold values from -6 to 6
- out_factors: bfloat16 [2048, 2, 512, 256], P(('feat', 'pair')), may hold values from -0.26367188 to 0.26367188
- token_counts: int32 [2048, 2], P(('feat', 'pair')), may hold values from 1 to 512, as said below
- slot_pair: int32 [4, 512], P('pair'), may hold values from 0 to 511, each once within a row
- factor_panels: float32 [65536, 1536], P('feat'), as said below
Outputs:
- reduced: float32 [2048, 65536], P('pair', 'feat')
The draws below stay inside these ranges and needn't reach their ends.
Inputs may be any that keep to these rules, and one draw needn't show every extreme that they name: `token_counts`: column 0 counts the chosen response's tokens, column 1 the rejected one's; positions at or beyond the count are padding. `slot_pair`: each row is a permutation of 0 to 511. `factor_panels`: entries above the diagonal in the unknowns' order are zero: rows of panel j hold zeros in the columns of panels after j, and D_k has a positive diagonal.
All inputs are finite; a program needn't handle non-finite values.
Results may differ from the reference program's by a relative error of at most 0.0003.
Values sent between devices are 32-bit elements; how exact they have to be, the bound alone decides.
No kernel may reach another device: no remote copies, remote signals or barrier semaphores. Data moves between devices by JAX's collectives and lax.ppermute only.
A program may use at most 128 MiB of HBM per device.

```python
import jax
import jax.numpy as jnp
from jax import lax

R = 256
F = 65536
LMAX = 512
PAIR_SUB = 4
PANEL = 512
PANELS = 3
BLOCKS = 32
GROUPS = 4
SLOTS = 16
PG = 512
PAIRS = 2048
ROWS_DEV = 2048


def draw_token_counts(key, part):
    key_counts, key_full, key_side, key_short = jax.random.split(jax.random.fold_in(key, 11), 4)
    counts = jax.random.randint(key_counts, (PAIRS, 2), 1, LMAX + 1)
    full_row = jax.random.randint(key_full, (), 0, PAIRS)
    full_side = jax.random.randint(key_side, (), 0, 2)
    short_row = (full_row + 1 + jax.random.randint(key_short, (), 0, PAIRS - 1)) % PAIRS
    row_index = lax.broadcasted_iota(jnp.int32, (PAIRS, 2), 0)
    side_index = lax.broadcasted_iota(jnp.int32, (PAIRS, 2), 1)
    counts = jnp.where((row_index == short_row) & (side_index == full_side), 1, counts)
    counts = jnp.where((row_index == full_row) & (side_index == full_side), LMAX, counts)
    return counts.astype(jnp.int32)


def draw_factor_panels(key, part):
    key_noise, key_diag = jax.random.split(jax.random.fold_in(key, 23), 2)
    shape = (F, PANELS * PANEL)
    row_index = lax.broadcasted_iota(jnp.int32, shape, 0)
    col_index = lax.broadcasted_iota(jnp.int32, shape, 1)
    block_index = row_index // (F // BLOCKS)
    offset = row_index % (F // BLOCKS)
    row_panel = jnp.where((block_index < PANELS) & (offset < PANEL), block_index, PANELS)
    col_panel = col_index // PANEL
    col_offset = col_index % PANEL
    noise = jax.random.normal(key_noise, shape, jnp.float32)
    diag_values = jax.random.uniform(key_diag, shape, jnp.float32, 1.0, 2.0)
    inside = row_panel == col_panel
    lower = inside & (offset > col_offset)
    on_diag = inside & (offset == col_offset)
    below = row_panel > col_panel
    values = jnp.where(below, noise / jnp.sqrt(jnp.float32(PANELS * PANEL)), 0.0)
    values = jnp.where(lower, noise * 0.6 / jnp.sqrt(jnp.float32(PANEL)), values)
    values = jnp.where(on_diag, diag_values, values)
    return values.astype(jnp.float32)


def block_scale(rng, shape, cuts, low, high):
    loudness = 1.0
    for dim, shards_of in cuts:
        draws = jax.random.uniform(jax.random.fold_in(jax.random.fold_in(rng, 6), dim), (shards_of,), jnp.float32, low / len(cuts), high / len(cuts))
        loudness = loudness * jnp.repeat(jnp.exp(draws), shape[dim] // shards_of).reshape((-1,) + (1,) * (len(shape) - 1 - dim))
    return loudness


def normal_values(stream_key, dims, width, most, cuts=(), held_as=jnp.bfloat16):
    drawn = jax.random.normal(stream_key, dims, jnp.float32) * width
    if len(cuts) > 0:
        drawn = block_scale(stream_key, dims, cuts, -0.22, 0.18) * drawn
    return jnp.clip(drawn, min=-most, max=most).astype(held_as)


def setup_inputs(seed: int = 0) -> dict:
    key_of = jax.random.split(jax.random.key(seed), 6)
    in_factors = normal_values(key_of[0], (PAIRS, 2, LMAX, R), 1.0, 6.0, ((0, 128),))
    out_factors = normal_values(key_of[1], (PAIRS, 2, LMAX, R), (LMAX ** -0.5), 0.26367188, ((0, 128),))
    token_counts = draw_token_counts(jax.random.fold_in(key_of[5], 71), 0)
    slot_pair = jax.vmap(lambda own: jax.random.permutation(own, PG))(jax.random.split(key_of[3], GROUPS)).reshape((GROUPS, PG)).astype(jnp.int32)
    factor_panels = draw_factor_panels(jax.random.fold_in(key_of[5], 71), 0)
    return {"in_factors": in_factors, "out_factors": out_factors, "token_counts": token_counts, "slot_pair": slot_pair, "factor_panels": factor_panels}


def block_gradients(pieces):
    signed_block, input_block = pieces
    result = jnp.einsum('ksti,kstj->kij', signed_block.astype(jnp.float32), input_block.astype(jnp.float32), precision=lax.Precision.HIGHEST)
    return result.reshape(signed_block.shape[0], R * R)

def reference(in_factors, out_factors, token_counts, slot_pair, factor_panels):
    positions = lax.broadcasted_iota(jnp.int32, (PAIRS, 2, LMAX), 2)
    side_index = lax.broadcasted_iota(jnp.int32, (PAIRS, 2, LMAX), 1)
    weights = jnp.where(positions < token_counts[:, :, None], jnp.where(side_index == 0, 1.0, -1.0), 0.0).astype(jnp.bfloat16)
    signed = out_factors * weights[..., None]
    blocked = (signed.reshape(PAIRS // SLOTS, SLOTS, 2, LMAX, R), in_factors.reshape(PAIRS // SLOTS, SLOTS, 2, LMAX, R))
    gradients = lax.map(block_gradients, blocked).reshape(PAIRS, R * R)
    ordered = gradients.reshape(BLOCKS, GROUPS, GROUPS, PAIR_SUB, R * R).transpose(2, 0, 1, 3, 4).reshape(GROUPS, PG, R * R)
    group_index = lax.broadcasted_iota(jnp.int32, (GROUPS, PG), 0)
    right_side = jnp.zeros((GROUPS, PG, R * R), jnp.float32).at[group_index, slot_pair].set(ordered).reshape(PAIRS, R * R)
    for k in range(PANELS):
        start = k * ROWS_DEV
        panel_cols = factor_panels[:, k * PANEL:(k + 1) * PANEL]
        diagonal = panel_cols[start:start + PANEL]
        solved = jax.scipy.linalg.solve_triangular(diagonal, right_side[:, start:start + PANEL].T, lower=True).T
        update = jnp.dot(solved.astype(jnp.float32), panel_cols.T.astype(jnp.float32), precision=lax.Precision.HIGHEST, preferred_element_type=jnp.float32)
        right_side = right_side - update
        right_side = right_side.at[:, start:start + PANEL].set(solved)
    return right_side
```

```python
import jax
import jax.numpy as jnp
from jax import lax
from jax.experimental import pallas as pl
from jax.experimental.pallas import tpu as pltpu
from jax.sharding import PartitionSpec as P

PANEL = 512
PANELS = 3
HIGH = lax.Precision.HIGH
HIGHEST = lax.Precision.HIGHEST


def gradient_kernel(counts_ref, out_ref, in_ref, send_ref, panel_ref):
    slot = pl.program_id(0)
    total = None
    for side in range(2):
        count = counts_ref[slot, side]
        factors = out_ref[0, side]
        position = lax.broadcasted_iota(jnp.int32, factors.shape, 0)
        kept = jnp.where(position < count, factors.astype(jnp.float32), 0.0).astype(jnp.bfloat16)
        product = lax.dot_general(
            kept, in_ref[0, side], (((0,), (0,)), ((), ())), preferred_element_type=jnp.float32
        )
        total = product if side == 0 else total - product
    rank = total.shape[1]
    send_ref[...] = total.reshape(send_ref.shape)
    for k in range(PANELS):
        panel_ref[0, 2 * k : 2 * k + 2, :] = total[8 * k : 8 * k + 2, :]
    panel_ref[0, 2 * PANELS :, :] = jnp.zeros((8 - 2 * PANELS, rank), jnp.float32)


def slot_gradients(token_counts, out_factors, in_factors, n_feat, n_pair):
    slots, sides, depth, rank = in_factors.shape
    per_group = slots // n_pair
    factors = pl.BlockSpec((1, sides, depth, rank), lambda k, counts: (k, 0, 0, 0))
    return pl.pallas_call(
        gradient_kernel,
        grid_spec=pltpu.PrefetchScalarGridSpec(
            num_scalar_prefetch=1,
            grid=(slots,),
            in_specs=[factors, factors],
            out_specs=[
                pl.BlockSpec(
                    (n_feat, 1, 1, rank // n_feat, rank),
                    lambda k, counts: (0, k // per_group, k % per_group, 0, 0),
                ),
                pl.BlockSpec((1, 8, rank), lambda k, counts: (k, 0, 0)),
            ],
        ),
        out_shape=[
            jax.ShapeDtypeStruct((n_feat, n_pair, per_group, rank // n_feat, rank), jnp.float32),
            jax.ShapeDtypeStruct((slots, 8, rank), jnp.float32),
        ],
        compiler_params=pltpu.CompilerParams(vmem_limit_bytes=48 * 2**20),
        name="slot_gradients",
    )(token_counts, out_factors, in_factors)


def invert_kernel(d_ref, x_ref):
    def dot(a, b):
        return jnp.dot(a, b, precision=HIGHEST, preferred_element_type=jnp.float32)

    base = 128
    count = PANEL // base
    row = lax.broadcasted_iota(jnp.int32, (base, base), 0)
    col = lax.broadcasted_iota(jnp.int32, (base, base), 1)
    blocks = [d_ref[n * base : (n + 1) * base, n * base : (n + 1) * base] for n in range(count)]
    inverses = [jnp.where(row == col, 1.0 / jnp.where(row == col, b, 1.0), 0.0) for b in blocks]
    size = 1
    while size < base:
        joins = (row // (2 * size) == col // (2 * size)) & (row // size != col // size) & (row > col)
        inner = [dot(jnp.where(joins, b, 0.0), x) for b, x in zip(blocks, inverses)]
        inverses = [x - dot(x, y) for x, y in zip(inverses, inner)]
        size *= 2
    x_ref[...] = jnp.zeros_like(x_ref)
    for n in range(count):
        x_ref[n * base : (n + 1) * base, n * base : (n + 1) * base] = inverses[n]
    size = base
    while size < PANEL:
        for start in range(0, PANEL, 2 * size):
            top = slice(start, start + size)
            low = slice(start + size, start + 2 * size)
            x_ref[low, top] = -dot(x_ref[low, low], dot(d_ref[low, top], x_ref[top, top]))
        size *= 2


def invert_lower(diagonal):
    return pl.pallas_call(
        invert_kernel,
        out_shape=jax.ShapeDtypeStruct(diagonal.shape, jnp.float32),
        compiler_params=pltpu.CompilerParams(vmem_limit_bytes=32 * 2**20),
        name="invert_lower",
    )(diagonal)


def place_kernel(owner_ref, pairs_ref, received_ref, update_ref, out_ref, high_ref, low_ref):
    step = pl.program_id(0)
    rows = out_ref.shape[0]
    total, parts, rank = received_ref.shape

    @pl.when(step == 0)
    def _():
        for i in range(parts):
            value = received_ref[:, i, :]
            if i * rank < PANEL:
                value = jnp.where(owner_ref[0] == 1, 0.0, value)
            high = value.astype(jnp.bfloat16)
            high_ref[i] = high
            low_ref[i] = (value - high.astype(jnp.float32)).astype(jnp.bfloat16)

    pair = lax.broadcasted_iota(jnp.int32, (rows, total), 0) + step * rows
    chosen = jnp.where(pair == pairs_ref[...], 1.0, 0.0).astype(jnp.bfloat16)
    for i in range(parts):
        placed = jnp.dot(chosen, high_ref[i], preferred_element_type=jnp.float32)
        placed += jnp.dot(chosen, low_ref[i], preferred_element_type=jnp.float32)
        columns = slice(i * rank, (i + 1) * rank)
        out_ref[:, columns] = placed - update_ref[:, columns]


def place_rows(owner, slot_pair, received, update):
    total, parts, rank = received.shape
    rows = 128
    return pl.pallas_call(
        place_kernel,
        grid=(total // rows,),
        in_specs=[
            pl.BlockSpec(memory_space=pltpu.SMEM),
            pl.BlockSpec((1, total), lambda i: (0, 0)),
            pl.BlockSpec((total, parts, rank), lambda i: (0, 0, 0)),
            pl.BlockSpec((rows, parts * rank), lambda i: (i, 0)),
        ],
        out_specs=pl.BlockSpec((rows, parts * rank), lambda i: (i, 0)),
        out_shape=jax.ShapeDtypeStruct((total, parts * rank), jnp.float32),
        scratch_shapes=[
            pltpu.VMEM((parts, total, rank), jnp.bfloat16),
            pltpu.VMEM((parts, total, rank), jnp.bfloat16),
        ],
        compiler_params=pltpu.CompilerParams(vmem_limit_bytes=48 * 2**20),
        name="place_rows",
    )(owner, slot_pair, received, update)


def times_transposed(a, b):
    return lax.dot_general(
        a, b, (((1,), (1,)), ((), ())), precision=HIGH, preferred_element_type=jnp.float32
    )


def gather_factor(factor_panels, inverse, feat, pair, n_feat, n_pair):
    units = n_feat // 2 * n_pair
    depth = PANEL // units
    core = feat % 2
    rows = factor_panels[:PANEL]
    quarter = lambda v: lax.dynamic_index_in_dim(
        v.reshape(n_feat // 2, n_pair, depth, v.shape[1]), pair, 1, keepdims=False
    )
    diag = quarter(inverse)
    below = quarter(rows[:, : 2 * PANEL])
    diag = jnp.concatenate([diag, jnp.zeros_like(diag)], axis=2)
    outgoing = jnp.stack([diag, below], axis=1).reshape(n_feat, depth, 2 * PANEL)
    arrived = lax.all_to_all(outgoing, "feat", split_axis=0, concat_axis=0, tiled=True)
    first = jnp.concatenate([arrived[k, :, :PANEL] for k in range(3)], axis=1)
    second = jnp.concatenate([arrived[1, :, :PANEL], arrived[2]], axis=1)
    shard = jnp.where(core == 0, first, second)
    groups = [
        [f * n_pair + p for f in range(c, n_feat, 2) for p in range(n_pair)] for c in range(2)
    ]
    mine = lax.all_gather(shard, ("feat", "pair"), axis_index_groups=groups, tiled=True)
    other = lax.ppermute(mine, "feat", [(f, f ^ 1) for f in range(n_feat)])
    inverses = jnp.where(core == 0, mine, other)
    belows = jnp.where(core == 0, other, mine)
    return inverses, belows


def per_device(in_factors, out_factors, token_counts, slot_pair, factor_panels):
    slots, _, _, rank = in_factors.shape
    n_pair = lax.axis_size("pair")
    n_feat = lax.axis_size("feat")
    per_group = slots // n_pair
    feat = lax.axis_index("feat")
    pair = lax.axis_index("pair")
    total = n_feat * slots

    panel_of = jnp.minimum(feat, PANELS - 1)
    diagonal = lax.dynamic_slice(factor_panels, (0, panel_of * PANEL), (PANEL, PANEL))
    diagonal = jnp.where(feat < PANELS, diagonal, jnp.eye(PANEL, dtype=jnp.float32))
    inverse = invert_lower(diagonal)
    inverses, belows = gather_factor(factor_panels, inverse, feat, pair, n_feat, n_pair)

    send, panel_part = slot_gradients(token_counts, out_factors, in_factors, n_feat, n_pair)
    received = lax.all_to_all(
        send.reshape(n_feat * n_pair, per_group, rank // n_feat, rank),
        ("feat", "pair"),
        split_axis=0,
        concat_axis=0,
        tiled=True,
    ).reshape(total, rank // n_feat, rank)

    panel_part = panel_part[:, : 2 * PANELS].reshape(n_pair, per_group, PANELS * PANEL)
    panel_part = lax.all_to_all(panel_part, "pair", split_axis=0, concat_axis=0, tiled=True)
    panel_rows = lax.all_gather(
        panel_part.reshape(slots, PANELS * PANEL), "feat", axis=0, tiled=True
    )
    pair_rows = lax.broadcasted_iota(jnp.int32, (total, total), 0)
    placement = (pair_rows == slot_pair).astype(jnp.float32)
    right = jnp.dot(placement, panel_rows, precision=HIGH, preferred_element_type=jnp.float32)

    inv = [inverses[:, k * PANEL : (k + 1) * PANEL] for k in range(PANELS)]
    low = [belows[:, k * PANEL : (k + 1) * PANEL] for k in range(PANELS)]
    rhs = [right[:, k * PANEL : (k + 1) * PANEL] for k in range(PANELS)]
    x0 = times_transposed(rhs[0], inv[0])
    x1 = times_transposed(rhs[1] - times_transposed(x0, low[0]), inv[1])
    x2 = times_transposed(
        rhs[2] - times_transposed(x0, low[1]) - times_transposed(x1, low[2]), inv[2]
    )
    solved = jnp.concatenate([x0, x1, x2], axis=1)
    update = times_transposed(solved, factor_panels)
    own = jnp.where(feat == 0, x0, jnp.where(feat == 1, x1, x2))
    is_owner = feat < PANELS
    update = update.at[:, :PANEL].set(jnp.where(is_owner, -own, update[:, :PANEL]))
    owner = is_owner.astype(jnp.int32).reshape(1)
    return place_rows(owner, slot_pair, received, update)


def solution(mesh):
    return jax.shard_map(
        per_device,
        mesh=mesh,
        in_specs=(
            P(("feat", "pair"), None, None, None),
            P(("feat", "pair"), None, None, None),
            P(("feat", "pair"), None),
            P("pair", None),
            P("feat", None),
        ),
        out_specs=P("pair", "feat"),
        check_vma=False,
    )
```

```python
import jax
import jax.numpy as jnp
from jax import lax
from jax.experimental import pallas as pl
from jax.experimental.pallas import tpu as pltpu
from jax.sharding import PartitionSpec as P

PANEL = 512
PANELS = 3
HIGHEST = lax.Precision.HIGHEST


def gradient_kernel(counts_ref, out_ref, in_ref, send_ref, panel_ref):
    slot = pl.program_id(0)
    depth, rank = out_ref.shape[2:]
    position = lax.broadcasted_iota(jnp.int32, (depth, 128), 0)
    total = None
    for side in range(2):
        kept = jnp.where(position < counts_ref[slot, side], 1.0, 0.0).astype(jnp.bfloat16)
        weights = jnp.concatenate([kept] * (rank // 128), axis=1)
        product = lax.dot_general(
            out_ref[0, side] * weights,
            in_ref[0, side],
            (((0,), (0,)), ((), ())),
            preferred_element_type=jnp.float32,
        )
        total = product if side == 0 else total - product
    feats, _, _, lanes, parts, lane = send_ref.shape
    for h in range(lanes):
        columns = total[:, h * lane : (h + 1) * lane]
        send_ref[:, 0, 0, h] = columns.reshape(feats, parts, lane)
    for k in range(PANELS):
        for i in range(PANEL // rank):
            columns = slice(k * PANEL + i * rank, k * PANEL + (i + 1) * rank)
            panel_ref[pl.ds(slot, 1), columns] = total[8 * k + i : 8 * k + i + 1, :]


def slot_gradients(token_counts, out_factors, in_factors, n_feat, n_pair):
    slots, sides, depth, rank = in_factors.shape
    per_group = slots // n_pair
    factors = pl.BlockSpec((1, sides, depth, rank), lambda k, counts: (k, 0, 0, 0))
    return pl.pallas_call(
        gradient_kernel,
        grid_spec=pltpu.PrefetchScalarGridSpec(
            num_scalar_prefetch=1,
            grid=(slots,),
            in_specs=[factors, factors],
            out_specs=[
                pl.BlockSpec(
                    (n_feat, 1, 1, rank // 128, rank // n_feat, 128),
                    lambda k, counts: (0, k // per_group, k % per_group, 0, 0, 0),
                ),
                pl.BlockSpec((slots, PANELS * PANEL), lambda k, counts: (0, 0)),
            ],
        ),
        out_shape=[
            jax.ShapeDtypeStruct(
                (n_feat, n_pair, per_group, rank // 128, rank // n_feat, 128), jnp.float32
            ),
            jax.ShapeDtypeStruct((slots, PANELS * PANEL), jnp.float32),
        ],
        compiler_params=pltpu.CompilerParams(vmem_limit_bytes=48 * 2**20),
        cost_estimate=pl.CostEstimate(
            flops=2 * slots * sides * depth * rank * rank, bytes_accessed=24 * 2**20, transcendentals=0
        ),
        name="slot_gradients",
    )(token_counts, out_factors, in_factors)


def invert_kernel(place_ref, panel_ref, send_ref, d_ref, x_ref):
    def dot(a, b):
        return jnp.dot(a, b, precision=HIGHEST, preferred_element_type=jnp.float32)

    whole_row = lax.broadcasted_iota(jnp.int32, d_ref.shape, 0)
    whole_col = lax.broadcasted_iota(jnp.int32, d_ref.shape, 1)
    d_ref[...] = jnp.where(whole_row == whole_col, 1.0, 0.0)
    for k in range(PANELS):

        @pl.when((place_ref[1] == 1) & (place_ref[0] == k))
        def _():
            d_ref[...] = panel_ref[:, k * PANEL : (k + 1) * PANEL]

    base = 128
    count = PANEL // base
    row = lax.broadcasted_iota(jnp.int32, (base, base), 0)
    col = lax.broadcasted_iota(jnp.int32, (base, base), 1)
    blocks = [d_ref[n * base : (n + 1) * base, n * base : (n + 1) * base] for n in range(count)]
    inverses = [jnp.where(row == col, 1.0 / jnp.where(row == col, b, 1.0), 0.0) for b in blocks]
    size = 1
    while size < base:
        joins = (row // (2 * size) == col // (2 * size)) & (row // size != col // size) & (row > col)
        inner = [dot(jnp.where(joins, b, 0.0), x) for b, x in zip(blocks, inverses)]
        inverses = [x - dot(x, y) for x, y in zip(inverses, inner)]
        size *= 2
    x_ref[...] = jnp.zeros_like(x_ref)
    for n in range(count):
        x_ref[n * base : (n + 1) * base, n * base : (n + 1) * base] = inverses[n]
    size = base
    while size < PANEL:
        for start in range(0, PANEL, 2 * size):
            top = slice(start, start + size)
            low = slice(start + size, start + 2 * size)
            x_ref[low, top] = -dot(x_ref[low, low], dot(d_ref[low, top], x_ref[top, top]))
        size *= 2
    chips, _, depth, _ = send_ref.shape
    groups = PANEL // (chips * depth)
    for chip in range(chips):
        rows = pl.ds(pl.multiple_of((chip * groups + place_ref[3]) * depth, depth), depth)
        send_ref[chip, 0, :, :PANEL] = x_ref[rows, :]
        send_ref[chip, 0, :, PANEL:] = jnp.zeros((depth, PANEL), jnp.float32)
        send_ref[chip, 1] = panel_ref[rows, : 2 * PANEL]


def invert_and_cut(place, factor_panels, n_feat, n_pair):
    width = factor_panels.shape[1]
    chips = n_feat // 2
    depth = PANEL // (chips * n_pair)
    return pl.pallas_call(
        invert_kernel,
        grid=(1,),
        in_specs=[
            pl.BlockSpec(memory_space=pltpu.SMEM),
            pl.BlockSpec((PANEL, width), lambda i: (0, 0)),
        ],
        out_specs=pl.BlockSpec((chips, 2, depth, 2 * PANEL), lambda i: (0, 0, 0, 0)),
        out_shape=jax.ShapeDtypeStruct((chips, 2, depth, 2 * PANEL), jnp.float32),
        scratch_shapes=[
            pltpu.VMEM((PANEL, PANEL), jnp.float32),
            pltpu.VMEM((PANEL, PANEL), jnp.float32),
        ],
        compiler_params=pltpu.CompilerParams(vmem_limit_bytes=60 * 2**20),
        name="invert_and_cut",
    )(place, factor_panels)


def split(value):
    high = value.astype(jnp.bfloat16)
    return high, (value - high.astype(jnp.float32)).astype(jnp.bfloat16)


def one_hot(pairs, first, rows):
    pair = lax.broadcasted_iota(jnp.int32, (rows, pairs.shape[1]), 0) + first
    return jnp.where(pair == pairs, 1.0, 0.0).astype(jnp.bfloat16)


def place_kernel(place_ref, pairs_ref, received_ref, update_ref, out_ref, high_ref, low_ref):
    step = pl.program_id(0)
    rows = out_ref.shape[0]
    parts, total, rank = high_ref.shape

    @pl.when(step == 0)
    def _():
        for i in range(parts):
            lanes = rank // 128
            value = jnp.concatenate(
                [
                    received_ref[pl.ds(h * parts + i, total, stride=lanes * parts), :]
                    for h in range(lanes)
                ],
                axis=1,
            )
            if i * rank < PANEL:
                value = jnp.where(place_ref[1] == 1, 0.0, value)
            high_ref[i], low_ref[i] = split(value)

    chosen = one_hot(pairs_ref[...], step * rows, rows)
    for i in range(parts):
        placed = jnp.dot(chosen, high_ref[i], preferred_element_type=jnp.float32)
        placed += jnp.dot(chosen, low_ref[i], preferred_element_type=jnp.float32)
        columns = slice(i * rank, (i + 1) * rank)
        out_ref[:, columns] = placed - update_ref[:, columns]


def place_rows(place, slot_pair, received, update):
    total, width = update.shape
    rank = 2 * received.shape[1]
    parts = width // rank
    rows = 128
    return pl.pallas_call(
        place_kernel,
        grid=(total // rows,),
        in_specs=[
            pl.BlockSpec(memory_space=pltpu.SMEM),
            pl.BlockSpec((1, total), lambda i: (0, 0)),
            pl.BlockSpec(received.shape, lambda i: (0, 0)),
            pl.BlockSpec((rows, width), lambda i: (i, 0)),
        ],
        out_specs=pl.BlockSpec((rows, width), lambda i: (i, 0)),
        out_shape=jax.ShapeDtypeStruct((total, width), jnp.float32),
        scratch_shapes=[
            pltpu.VMEM((parts, total, rank), jnp.bfloat16),
            pltpu.VMEM((parts, total, rank), jnp.bfloat16),
        ],
        compiler_params=pltpu.CompilerParams(vmem_limit_bytes=48 * 2**20),
        name="place_rows",
    )(place, slot_pair, received, update)


def dot_split(a, b):
    def dot(x, y):
        return lax.dot_general(x, y, (((1,), (1,)), ((), ())), preferred_element_type=jnp.float32)

    return dot(a[0], b[0]) + (dot(a[0], b[1]) + dot(a[1], b[0]))


def arrange_kernel(pairs_ref, near_ref, far_ref, out_ref):
    half = near_ref.shape[0]
    right = None
    for n, ref in enumerate((near_ref, far_ref)):
        chosen = one_hot(pairs_ref[:, n * half : (n + 1) * half], 0, 2 * half)
        for part in split(ref[...]):
            moved = jnp.dot(chosen, part, preferred_element_type=jnp.float32)
            right = moved if right is None else right + moved
    out_ref[...] = right


def arrange_rows(pairs, near, far):
    half, width = near.shape
    rows = pl.BlockSpec((half, PANEL), lambda k: (0, k))
    return pl.pallas_call(
        arrange_kernel,
        grid=(width // PANEL,),
        in_specs=[pl.BlockSpec(pairs.shape, lambda k: (0, 0)), rows, rows],
        out_specs=pl.BlockSpec((2 * half, PANEL), lambda k: (0, k)),
        out_shape=jax.ShapeDtypeStruct((2 * half, width), jnp.float32),
        compiler_params=pltpu.CompilerParams(vmem_limit_bytes=40 * 2**20),
        name="arrange_rows",
    )(pairs, near, far)


def split_kernel(value_ref, high_ref, low_ref):
    high_ref[...], low_ref[...] = split(value_ref[...])


def split_factor(factor_panels):
    rows, depth = factor_panels.shape
    block = pl.BlockSpec((256, depth), lambda i: (i, 0))
    return pl.pallas_call(
        split_kernel,
        grid=(rows // 256,),
        in_specs=[block],
        out_specs=[block, block],
        out_shape=[jax.ShapeDtypeStruct((rows, depth), jnp.bfloat16)] * 2,
        compiler_params=pltpu.CompilerParams(vmem_limit_bytes=60 * 2**20),
        name="split_factor",
    )(factor_panels)


def solve_kernel(
    place_ref, right_ref, mine_ref, other_ref, factor_high_ref, factor_low_ref, out_ref,
    solved_ref, high_ref, low_ref,
):
    step = pl.program_id(0)
    width = out_ref.shape[1]

    @pl.when(step == 0)
    def _():
        first_core = place_ref[2] == 0

        def factor(k, below):
            columns = slice(k * PANEL, (k + 1) * PANEL)
            return split(
                jnp.where(first_core != below, mine_ref[:, columns], other_ref[:, columns])
            )

        for k in range(PANELS):
            columns = slice(k * PANEL, (k + 1) * PANEL)
            right = right_ref[:, columns]
            for j in range(k):
                before = slice(j * PANEL, (j + 1) * PANEL)
                solved = (high_ref[:, before], low_ref[:, before])
                right -= dot_split(solved, factor(k * (k - 1) // 2 + j, True))
            value = dot_split(split(right), factor(k, False))
            solved_ref[k] = value
            high_ref[:, columns], low_ref[:, columns] = split(value)

    out_ref[...] = dot_split(
        (high_ref[...], low_ref[...]), (factor_high_ref[...], factor_low_ref[...])
    )

    for i in range(PANEL // width):

        @pl.when((place_ref[1] == 1) & (step == i))
        def _():
            out_ref[...] = -solved_ref[place_ref[0], :, i * width : (i + 1) * width]


def solve_and_update(place, right, mine, other, factor_parts):
    rows, depth = factor_parts[0].shape
    total = right.shape[0]
    width = 256
    whole = lambda v: pl.BlockSpec(v.shape, lambda i: (0, 0))
    block = pl.BlockSpec((width, depth), lambda i: (i, 0))
    return pl.pallas_call(
        solve_kernel,
        grid=(rows // width,),
        in_specs=[
            pl.BlockSpec(memory_space=pltpu.SMEM),
            whole(right),
            whole(mine),
            whole(other),
            block,
            block,
        ],
        out_specs=pl.BlockSpec((total, width), lambda i: (0, i)),
        out_shape=jax.ShapeDtypeStruct((total, rows), jnp.float32),
        scratch_shapes=[
            pltpu.VMEM((PANELS, total, PANEL), jnp.float32),
            pltpu.VMEM((total, depth), jnp.bfloat16),
            pltpu.VMEM((total, depth), jnp.bfloat16),
        ],
        compiler_params=pltpu.CompilerParams(vmem_limit_bytes=48 * 2**20),
        name="solve_and_update",
    )(place, right, mine, other, *factor_parts)


def gather_factor(arrived, feat, n_feat, n_pair):
    first = jnp.concatenate([arrived[k, :, :PANEL] for k in range(3)], axis=1)
    second = jnp.concatenate([arrived[1, :, :PANEL], arrived[2]], axis=1)
    shard = jnp.where(feat % 2 == 0, first, second)
    groups = [
        [f * n_pair + p for f in range(c, n_feat, 2) for p in range(n_pair)] for c in range(2)
    ]
    return lax.all_gather(shard, ("feat", "pair"), axis_index_groups=groups, tiled=True)


def along(value, axis, shift):
    if axis == "pair":
        return lax.ppermute(value, "pair", [(p, (p + shift) % 4) for p in range(4)])
    stride = 8 if axis == "y" else 2
    ring = lambda f: f - f // stride % 4 * stride + (f // stride + shift) % 4 * stride
    n_feat = lax.axis_size("feat")
    return lax.ppermute(value, "feat", [(f, ring(f)) for f in range(n_feat)])


def gather_rows(panel_part, feat, pair, slot_pair):
    slots, width = panel_part.shape
    groups = panel_part.reshape(4, slots // 4, width)
    piece = lambda k: lax.dynamic_index_in_dim(groups, (pair + k) % 4, 0, keepdims=False)
    rows = jnp.concatenate([piece(0)] + [along(piece(k), "pair", k) for k in range(1, 4)], axis=0)
    half = slots // 2
    gathered = []
    for part, axes in ((rows[:half], ("z", "y")), (rows[half:], ("y", "z"))):
        for axis in axes:
            part = jnp.concatenate([part] + [along(part, axis, k) for k in range(1, 4)], axis=0)
        gathered.append(part)
    near = jnp.concatenate(gathered, axis=0)
    far = lax.ppermute(near, "feat", [(f, f ^ 1) for f in range(lax.axis_size("feat"))])
    n = lax.broadcasted_iota(jnp.int32, (128, 128), 0)
    other_core, second, outer, inner, back = n // 64, n // 32 % 2, n // 8 % 4, n // 2 % 4, n % 2
    y_back = jnp.where(second == 0, outer, inner)
    z_back = jnp.where(second == 0, inner, outer)
    y = (feat // 8 + 4 - y_back) % 4
    z = (feat // 2 % 4 + 4 - z_back) % 4
    core = (feat % 2 + other_core) % 2
    x = (pair + 4 - (2 * second + back)) % 4
    source = ((y * 4 + z) * 2 + core) * 4 + x
    chosen = (source == lax.broadcasted_iota(jnp.int32, (128, 128), 1)).astype(jnp.float32)
    table = slot_pair.reshape(128, slots // 4).astype(jnp.float32)
    pairs = jnp.dot(chosen, table, precision=HIGHEST, preferred_element_type=jnp.float32)
    pairs = jnp.round(pairs).astype(jnp.int32).reshape(1, 32 * slots)
    return near, far, pairs


def per_device(in_factors, out_factors, token_counts, slot_pair, factor_panels):
    slots, _, _, rank = in_factors.shape
    n_pair = lax.axis_size("pair")
    n_feat = lax.axis_size("feat")
    per_group = slots // n_pair
    feat = lax.axis_index("feat")
    pair = lax.axis_index("pair")
    total = n_feat * slots

    place = jnp.stack(
        [jnp.minimum(feat, PANELS - 1), (feat < PANELS).astype(jnp.int32), feat % 2, pair]
    ).astype(jnp.int32)
    outgoing = invert_and_cut(place, factor_panels, n_feat, n_pair)
    arrived = lax.all_to_all(
        outgoing.reshape((n_feat,) + outgoing.shape[2:]), "feat", split_axis=0, concat_axis=0, tiled=True
    )
    send, panel_part = slot_gradients(token_counts, out_factors, in_factors, n_feat, n_pair)
    arrived, panel_part = lax.optimization_barrier((arrived, panel_part))
    mine = gather_factor(arrived, feat, n_feat, n_pair)
    near, far, pairs = gather_rows(panel_part, feat, pair, slot_pair)
    send, near = lax.optimization_barrier((send, near))
    right = arrange_rows(pairs, near, far)
    parts = split_factor(factor_panels)
    mine, right, parts = lax.optimization_barrier((mine, right, parts))
    other = lax.ppermute(mine, "feat", [(f, f ^ 1) for f in range(n_feat)])
    received = lax.all_to_all(
        send.reshape((n_feat * n_pair,) + send.shape[2:]),
        ("feat", "pair"),
        split_axis=0,
        concat_axis=0,
        tiled=True,
    ).reshape(total * (rank // 128) * (rank // n_feat), 128)
    update = solve_and_update(place, right, mine, other, parts)
    return place_rows(place, slot_pair, received, update)


def solution(mesh):
    return jax.shard_map(
        per_device,
        mesh=mesh,
        in_specs=(
            P(("feat", "pair"), None, None, None),
            P(("feat", "pair"), None, None, None),
            P(("feat", "pair"), None),
            P("pair", None),
            P("feat", None),
        ),
        out_specs=P("pair", "feat"),
        check_vma=False,
    )
```

```python
import jax
import jax.numpy as jnp
from jax import lax
from jax.experimental import pallas as pl
from jax.experimental.pallas import tpu as pltpu
from jax.sharding import PartitionSpec as P

PANEL = 512
PANELS = 3
HIGHEST = lax.Precision.HIGHEST


def gradient_kernel(counts_ref, out_ref, in_ref, send_ref, panel_ref):
    slot = pl.program_id(0)
    depth, rank = out_ref.shape[2:]
    position = lax.broadcasted_iota(jnp.int32, (depth, 128), 0)
    total = None
    for side in range(2):
        kept = jnp.where(position < counts_ref[slot, side], 1.0, 0.0).astype(jnp.bfloat16)
        weights = jnp.concatenate([kept] * (rank // 128), axis=1)
        product = lax.dot_general(
            out_ref[0, side] * weights,
            in_ref[0, side],
            (((0,), (0,)), ((), ())),
            preferred_element_type=jnp.float32,
        )
        total = product if side == 0 else total - product
    feats, _, _, lanes, parts, lane = send_ref.shape
    for h in range(lanes):
        columns = total[:, h * lane : (h + 1) * lane]
        send_ref[:, 0, 0, h] = columns.reshape(feats, parts, lane)
    for k in range(PANELS):
        for i in range(PANEL // rank):
            columns = slice(k * PANEL + i * rank, k * PANEL + (i + 1) * rank)
            panel_ref[pl.ds(slot, 1), columns] = total[8 * k + i : 8 * k + i + 1, :]


def slot_gradients(token_counts, out_factors, in_factors, n_feat, n_pair):
    slots, sides, depth, rank = in_factors.shape
    per_group = slots // n_pair
    factors = pl.BlockSpec((1, sides, depth, rank), lambda k, counts: (k, 0, 0, 0))
    return pl.pallas_call(
        gradient_kernel,
        grid_spec=pltpu.PrefetchScalarGridSpec(
            num_scalar_prefetch=1,
            grid=(slots,),
            in_specs=[factors, factors],
            out_specs=[
                pl.BlockSpec(
                    (n_feat, 1, 1, rank // 128, rank // n_feat, 128),
                    lambda k, counts: (0, k // per_group, k % per_group, 0, 0, 0),
                ),
                pl.BlockSpec((slots, PANELS * PANEL), lambda k, counts: (0, 0)),
            ],
        ),
        out_shape=[
            jax.ShapeDtypeStruct(
                (n_feat, n_pair, per_group, rank // 128, rank // n_feat, 128), jnp.float32
            ),
            jax.ShapeDtypeStruct((slots, PANELS * PANEL), jnp.float32),
        ],
        compiler_params=pltpu.CompilerParams(vmem_limit_bytes=48 * 2**20),
        cost_estimate=pl.CostEstimate(
            flops=2 * slots * sides * depth * rank * rank, bytes_accessed=24 * 2**20, transcendentals=0
        ),
        name="slot_gradients",
    )(token_counts, out_factors, in_factors)


def invert_kernel(place_ref, panel_ref, send_ref, d_ref, x_ref):
    def dot(a, b):
        return jnp.dot(a, b, precision=HIGHEST, preferred_element_type=jnp.float32)

    whole_row = lax.broadcasted_iota(jnp.int32, d_ref.shape, 0)
    whole_col = lax.broadcasted_iota(jnp.int32, d_ref.shape, 1)
    d_ref[...] = jnp.where(whole_row == whole_col, 1.0, 0.0)
    for k in range(PANELS):

        @pl.when((place_ref[1] == 1) & (place_ref[0] == k))
        def _():
            d_ref[...] = panel_ref[:, k * PANEL : (k + 1) * PANEL]

    base = 128
    count = PANEL // base
    row = lax.broadcasted_iota(jnp.int32, (base, base), 0)
    col = lax.broadcasted_iota(jnp.int32, (base, base), 1)
    blocks = [d_ref[n * base : (n + 1) * base, n * base : (n + 1) * base] for n in range(count)]
    inverses = [jnp.where(row == col, 1.0 / jnp.where(row == col, b, 1.0), 0.0) for b in blocks]
    size = 1
    while size < base:
        joins = (row // (2 * size) == col // (2 * size)) & (row // size != col // size) & (row > col)
        inner = [dot(jnp.where(joins, b, 0.0), x) for b, x in zip(blocks, inverses)]
        inverses = [x - dot(x, y) for x, y in zip(inverses, inner)]
        size *= 2
    x_ref[...] = jnp.zeros_like(x_ref)
    for n in range(count):
        x_ref[n * base : (n + 1) * base, n * base : (n + 1) * base] = inverses[n]
    size = base
    while size < PANEL:
        for start in range(0, PANEL, 2 * size):
            top = slice(start, start + size)
            low = slice(start + size, start + 2 * size)
            x_ref[low, top] = -dot(x_ref[low, low], dot(d_ref[low, top], x_ref[top, top]))
        size *= 2
    chips, _, depth, _ = send_ref.shape
    groups = PANEL // (chips * depth)
    for chip in range(chips):
        rows = pl.ds(pl.multiple_of((chip * groups + place_ref[3]) * depth, depth), depth)
        send_ref[chip, 0, :, :PANEL] = x_ref[rows, :]
        send_ref[chip, 0, :, PANEL:] = jnp.zeros((depth, PANEL), jnp.float32)
        send_ref[chip, 1] = panel_ref[rows, : 2 * PANEL]


def invert_and_cut(place, factor_panels, n_feat, n_pair):
    width = factor_panels.shape[1]
    chips = n_feat // 2
    depth = PANEL // (chips * n_pair)
    return pl.pallas_call(
        invert_kernel,
        grid=(1,),
        in_specs=[
            pl.BlockSpec(memory_space=pltpu.SMEM),
            pl.BlockSpec((PANEL, width), lambda i: (0, 0)),
        ],
        out_specs=pl.BlockSpec((chips, 2, depth, 2 * PANEL), lambda i: (0, 0, 0, 0)),
        out_shape=jax.ShapeDtypeStruct((chips, 2, depth, 2 * PANEL), jnp.float32),
        scratch_shapes=[
            pltpu.VMEM((PANEL, PANEL), jnp.float32),
            pltpu.VMEM((PANEL, PANEL), jnp.float32),
        ],
        compiler_params=pltpu.CompilerParams(vmem_limit_bytes=60 * 2**20),
        name="invert_and_cut",
    )(place, factor_panels)


def split(value):
    high = value.astype(jnp.bfloat16)
    return high, (value - high.astype(jnp.float32)).astype(jnp.bfloat16)


def one_hot(pairs, first, rows):
    pair = lax.broadcasted_iota(jnp.int32, (rows, pairs.shape[1]), 0) + first
    return jnp.where(pair == pairs, 1.0, 0.0).astype(jnp.bfloat16)


def place_kernel(place_ref, pairs_ref, received_ref, update_ref, out_ref, high_ref, low_ref):
    step = pl.program_id(0)
    rows = out_ref.shape[0]
    parts, total, rank = high_ref.shape

    @pl.when(step == 0)
    def _():
        for i in range(parts):
            lanes = rank // 128
            value = jnp.concatenate(
                [
                    received_ref[pl.ds(h * parts + i, total, stride=lanes * parts), :]
                    for h in range(lanes)
                ],
                axis=1,
            )
            if i * rank < PANEL:
                value = jnp.where(place_ref[1] == 1, 0.0, value)
            high_ref[i], low_ref[i] = split(value)

    chosen = one_hot(pairs_ref[...], step * rows, rows)
    for i in range(parts):
        placed = jnp.dot(chosen, high_ref[i], preferred_element_type=jnp.float32)
        placed += jnp.dot(chosen, low_ref[i], preferred_element_type=jnp.float32)
        columns = slice(i * rank, (i + 1) * rank)
        out_ref[:, columns] = placed - update_ref[:, columns]


def place_rows(place, slot_pair, received, update):
    total, width = update.shape
    rank = 2 * received.shape[1]
    parts = width // rank
    rows = 128
    return pl.pallas_call(
        place_kernel,
        grid=(total // rows,),
        in_specs=[
            pl.BlockSpec(memory_space=pltpu.SMEM),
            pl.BlockSpec((1, total), lambda i: (0, 0)),
            pl.BlockSpec(received.shape, lambda i: (0, 0)),
            pl.BlockSpec((rows, width), lambda i: (i, 0)),
        ],
        out_specs=pl.BlockSpec((rows, width), lambda i: (i, 0)),
        out_shape=jax.ShapeDtypeStruct((total, width), jnp.float32),
        scratch_shapes=[
            pltpu.VMEM((parts, total, rank), jnp.bfloat16),
            pltpu.VMEM((parts, total, rank), jnp.bfloat16),
        ],
        compiler_params=pltpu.CompilerParams(vmem_limit_bytes=48 * 2**20),
        name="place_rows",
    )(place, slot_pair, received, update)


def dot_split(a, b):
    def dot(x, y):
        return lax.dot_general(x, y, (((1,), (1,)), ((), ())), preferred_element_type=jnp.float32)

    return dot(a[0], b[0]) + (dot(a[0], b[1]) + dot(a[1], b[0]))


def arrange_kernel(place_ref, pairs_ref, near_ref, far_ref, right_ref, panels_ref):
    blocks = near_ref.shape[0]
    half = blocks * 8
    core, pair, y, z = place_ref[2], place_ref[3], place_ref[4], place_ref[5]
    right = None
    for n, ref in enumerate((near_ref, far_ref)):
        chosen = one_hot(pairs_ref[:, n * half : (n + 1) * half], 0, 2 * half)
        for part in split(ref[:, 16:, :].reshape(half, PANEL)):
            moved = jnp.dot(chosen, part, preferred_element_type=jnp.float32)
            right = moved if right is None else right + moved
        kind = core if n == 0 else 1 - core
        for block in range(blocks):
            second, outer, inner = block // 16, block // 4 % 4, block % 4
            y_back, z_back = (outer, inner) if second == 0 else (inner, outer)
            chip = lax.rem(y + 4 - y_back, 4) * 4 + lax.rem(z + 4 - z_back, 4)
            for j in range(2):
                unit = chip * 4 + lax.rem(pair + 4 - (2 * second + j), 4)
                rows = pl.ds(pl.multiple_of(unit * 8, 8), 8)
                panels_ref[kind, rows, :] = ref[block, 8 * j : 8 * j + 8, :]
    right_ref[...] = right


def arrange_rows(place, pairs, near, far):
    blocks, depth, width = near.shape
    total = pairs.shape[1]
    rows = pl.BlockSpec((blocks, depth, PANEL), lambda k: (0, 0, k))
    return pl.pallas_call(
        arrange_kernel,
        grid=(width // PANEL,),
        in_specs=[
            pl.BlockSpec(memory_space=pltpu.SMEM),
            pl.BlockSpec(pairs.shape, lambda k: (0, 0)),
            rows,
            rows,
        ],
        out_specs=[
            pl.BlockSpec((total, PANEL), lambda k: (0, k)),
            pl.BlockSpec((2, PANEL, PANEL), lambda k: (0, 0, k)),
        ],
        out_shape=[
            jax.ShapeDtypeStruct((total, width), jnp.float32),
            jax.ShapeDtypeStruct((2, PANEL, width), jnp.float32),
        ],
        compiler_params=pltpu.CompilerParams(vmem_limit_bytes=40 * 2**20),
        name="arrange_rows",
    )(place, pairs, near, far)


def split_kernel(value_ref, high_ref, low_ref):
    high_ref[...], low_ref[...] = split(value_ref[...])


def split_factor(factor_panels):
    rows, depth = factor_panels.shape
    block = pl.BlockSpec((256, depth), lambda i: (i, 0))
    return pl.pallas_call(
        split_kernel,
        grid=(rows // 256,),
        in_specs=[block],
        out_specs=[block, block],
        out_shape=[jax.ShapeDtypeStruct((rows, depth), jnp.bfloat16)] * 2,
        compiler_params=pltpu.CompilerParams(vmem_limit_bytes=60 * 2**20),
        name="split_factor",
    )(factor_panels)


def solve_kernel(
    place_ref, right_ref, panels_ref, factor_high_ref, factor_low_ref, out_ref,
    solved_ref, high_ref, low_ref,
):
    step = pl.program_id(0)
    width = out_ref.shape[1]

    @pl.when(step == 0)
    def _():

        def factor(k, kind):
            return split(panels_ref[kind, :, k * PANEL : (k + 1) * PANEL])

        for k in range(PANELS):
            columns = slice(k * PANEL, (k + 1) * PANEL)
            right = right_ref[:, columns]
            for j in range(k):
                before = slice(j * PANEL, (j + 1) * PANEL)
                solved = (high_ref[:, before], low_ref[:, before])
                right -= dot_split(solved, factor(k * (k - 1) // 2 + j, 1))
            value = dot_split(split(right), factor(k, 0))
            solved_ref[k] = value
            high_ref[:, columns], low_ref[:, columns] = split(value)

    out_ref[...] = dot_split(
        (high_ref[...], low_ref[...]), (factor_high_ref[...], factor_low_ref[...])
    )

    for i in range(PANEL // width):

        @pl.when((place_ref[1] == 1) & (step == i))
        def _():
            out_ref[...] = -solved_ref[place_ref[0], :, i * width : (i + 1) * width]


def solve_and_update(place, right, panels, factor_parts):
    rows, depth = factor_parts[0].shape
    total = right.shape[0]
    width = 256
    whole = lambda v: pl.BlockSpec(v.shape, lambda i: (0, 0))
    block = pl.BlockSpec((width, depth), lambda i: (i, 0))
    return pl.pallas_call(
        solve_kernel,
        grid=(rows // width,),
        in_specs=[
            pl.BlockSpec(memory_space=pltpu.SMEM),
            whole(right),
            pl.BlockSpec(panels.shape, lambda i: (0, 0, 0)),
            block,
            block,
        ],
        out_specs=pl.BlockSpec((total, width), lambda i: (0, i)),
        out_shape=jax.ShapeDtypeStruct((total, rows), jnp.float32),
        scratch_shapes=[
            pltpu.VMEM((PANELS, total, PANEL), jnp.float32),
            pltpu.VMEM((total, depth), jnp.bfloat16),
            pltpu.VMEM((total, depth), jnp.bfloat16),
        ],
        compiler_params=pltpu.CompilerParams(vmem_limit_bytes=48 * 2**20),
        name="solve_and_update",
    )(place, right, panels, *factor_parts)


def along(value, axis, shift):
    if axis == "pair":
        return lax.ppermute(value, "pair", [(p, (p + shift) % 4) for p in range(4)])
    stride = 8 if axis == "y" else 2
    ring = lambda f: f - f // stride % 4 * stride + (f // stride + shift) % 4 * stride
    n_feat = lax.axis_size("feat")
    return lax.ppermute(value, "feat", [(f, ring(f)) for f in range(n_feat)])


def gather_panels(arrived, panel_part, send, feat, pair, slot_pair):
    slots, width = panel_part.shape
    first = jnp.concatenate([arrived[k, :, :PANEL] for k in range(3)], axis=1)
    second = jnp.concatenate([arrived[1, :, :PANEL], arrived[2]], axis=1)
    shard = jnp.where(feat % 2 == 0, first, second)
    depth = shard.shape[0]
    groups = panel_part.reshape(4, slots // 4, width)
    piece = lambda k: lax.dynamic_index_in_dim(groups, (pair + k) % 4, 0, keepdims=False)
    load = lambda k: jnp.concatenate([shard, piece(k)], axis=0)
    pieces = [load(0)] + [along(load(k), "pair", k) for k in range(1, 4)]
    halves = [
        jnp.concatenate([v[:depth] for v in two] + [v[depth:] for v in two], axis=0)[None]
        for two in (pieces[:2], pieces[2:])
    ]
    orders = (("z", "y"), ("y", "z"))
    ring = lambda part, axis: jnp.concatenate(
        [part] + [along(part, axis, k) for k in range(1, 4)], axis=0
    )
    halves = [ring(part, order[0]) for part, order in zip(halves, orders)]
    halves, send = lax.optimization_barrier((halves, send))
    near = jnp.concatenate([ring(part, order[1]) for part, order in zip(halves, orders)], axis=0)
    far = lax.ppermute(near, "feat", [(f, f ^ 1) for f in range(lax.axis_size("feat"))])
    n = lax.broadcasted_iota(jnp.int32, (128, 128), 0)
    other_core, second, outer, inner, back = n // 64, n // 32 % 2, n // 8 % 4, n // 2 % 4, n % 2
    y_back = jnp.where(second == 0, outer, inner)
    z_back = jnp.where(second == 0, inner, outer)
    y = (feat // 8 + 4 - y_back) % 4
    z = (feat // 2 % 4 + 4 - z_back) % 4
    core = (feat % 2 + other_core) % 2
    x = (pair + 4 - (2 * second + back)) % 4
    source = ((y * 4 + z) * 2 + core) * 4 + x
    chosen = (source == lax.broadcasted_iota(jnp.int32, (128, 128), 1)).astype(jnp.float32)
    table = slot_pair.reshape(128, slots // 4).astype(jnp.float32)
    pairs = jnp.dot(chosen, table, precision=HIGHEST, preferred_element_type=jnp.float32)
    pairs = jnp.round(pairs).astype(jnp.int32).reshape(1, 32 * slots)
    return near, far, pairs, send


def per_device(in_factors, out_factors, token_counts, slot_pair, factor_panels):
    slots, _, _, rank = in_factors.shape
    n_pair = lax.axis_size("pair")
    n_feat = lax.axis_size("feat")
    per_group = slots // n_pair
    feat = lax.axis_index("feat")
    pair = lax.axis_index("pair")
    total = n_feat * slots

    place = jnp.stack(
        [jnp.minimum(feat, PANELS - 1), (feat < PANELS).astype(jnp.int32), feat % 2, pair]
        + [feat // 8, feat // 2 % 4]
    ).astype(jnp.int32)
    outgoing = invert_and_cut(place, factor_panels, n_feat, n_pair)
    arrived = lax.all_to_all(
        outgoing.reshape((n_feat,) + outgoing.shape[2:]), "feat", split_axis=0, concat_axis=0, tiled=True
    )
    send, panel_part = slot_gradients(token_counts, out_factors, in_factors, n_feat, n_pair)
    arrived, panel_part = lax.optimization_barrier((arrived, panel_part))
    near, far, pairs, send = gather_panels(arrived, panel_part, send, feat, pair, slot_pair)
    received = lax.all_to_all(
        send.reshape((n_feat * n_pair,) + send.shape[2:]),
        ("feat", "pair"),
        split_axis=0,
        concat_axis=0,
        tiled=True,
    ).reshape(total * (rank // 128) * (rank // n_feat), 128)
    right, panels = arrange_rows(place, pairs, near, far)
    parts = split_factor(factor_panels)
    update = solve_and_update(place, right, panels, parts)
    return place_rows(place, slot_pair, received, update)


def solution(mesh):
    return jax.shard_map(
        per_device,
        mesh=mesh,
        in_specs=(
            P(("feat", "pair"), None, None, None),
            P(("feat", "pair"), None, None, None),
            P(("feat", "pair"), None),
            P("pair", None),
            P("feat", None),
        ),
        out_specs=P("pair", "feat"),
        check_vma=False,
    )
```

```python
import jax
import jax.numpy as jnp
from jax import lax
from jax.experimental import pallas as pl
from jax.experimental.pallas import tpu as pltpu
from jax.sharding import PartitionSpec as P

PANEL = 512
PANELS = 3
HIGHEST = lax.Precision.HIGHEST
SMALL = pl.CostEstimate(flops=1, bytes_accessed=1, transcendentals=0)


def gradient_kernel(counts_ref, out_ref, in_ref, send_ref, panel_ref):
    slot = pl.program_id(0)
    depth, rank = out_ref.shape[2:]
    position = lax.broadcasted_iota(jnp.int32, (depth, 128), 0)
    total = None
    for side in range(2):
        kept = jnp.where(position < counts_ref[slot, side], 1.0, 0.0).astype(jnp.bfloat16)
        weights = jnp.concatenate([kept] * (rank // 128), axis=1)
        product = lax.dot_general(
            out_ref[0, side] * weights,
            in_ref[0, side],
            (((0,), (0,)), ((), ())),
            preferred_element_type=jnp.float32,
        )
        total = product if side == 0 else total - product
    feats, _, _, lanes, parts, lane = send_ref.shape
    for h in range(lanes):
        columns = total[:, h * lane : (h + 1) * lane]
        send_ref[:, 0, 0, h] = columns.reshape(feats, parts, lane)
    for k in range(PANELS):
        for i in range(PANEL // rank):
            columns = slice(k * PANEL + i * rank, k * PANEL + (i + 1) * rank)
            panel_ref[pl.ds(slot, 1), columns] = total[8 * k + i : 8 * k + i + 1, :]


def slot_gradients(token_counts, out_factors, in_factors, n_feat, n_pair):
    slots, sides, depth, rank = in_factors.shape
    per_group = slots // n_pair
    factors = pl.BlockSpec((1, sides, depth, rank), lambda k, counts: (k, 0, 0, 0))
    return pl.pallas_call(
        gradient_kernel,
        grid_spec=pltpu.PrefetchScalarGridSpec(
            num_scalar_prefetch=1,
            grid=(slots,),
            in_specs=[factors, factors],
            out_specs=[
                pl.BlockSpec(
                    (n_feat, 1, 1, rank // 128, rank // n_feat, 128),
                    lambda k, counts: (0, k // per_group, k % per_group, 0, 0, 0),
                ),
                pl.BlockSpec((slots, PANELS * PANEL), lambda k, counts: (0, 0)),
            ],
        ),
        out_shape=[
            jax.ShapeDtypeStruct(
                (n_feat, n_pair, per_group, rank // 128, rank // n_feat, 128), jnp.float32
            ),
            jax.ShapeDtypeStruct((slots, PANELS * PANEL), jnp.float32),
        ],
        compiler_params=pltpu.CompilerParams(vmem_limit_bytes=60 * 2**20),
        cost_estimate=pl.CostEstimate(
            flops=2 * slots * sides * depth * rank * rank, bytes_accessed=24 * 2**20, transcendentals=0
        ),
        name="slot_gradients",
    )(token_counts, out_factors, in_factors)


def cut_kernel(place_ref, panel_ref, send_ref):
    chips, _, depth, _ = send_ref.shape
    groups = PANEL // (chips * depth)
    for chip in range(chips):
        rows = pl.ds(pl.multiple_of((chip * groups + place_ref[3]) * depth, depth), depth)
        diagonal = panel_ref[rows, (PANELS - 1) * PANEL :]
        for k in range(PANELS - 1):
            diagonal = jnp.where(
                place_ref[0] == k, panel_ref[rows, k * PANEL : (k + 1) * PANEL], diagonal
            )
        send_ref[chip, 0, :, :PANEL] = diagonal
        send_ref[chip, 0, :, PANEL:] = jnp.zeros((depth, PANEL), jnp.float32)
        send_ref[chip, 1] = panel_ref[rows, : 2 * PANEL]


def cut_panel(place, factor_panels, n_feat, n_pair):
    width = factor_panels.shape[1]
    chips = n_feat // 2
    depth = PANEL // (chips * n_pair)
    return pl.pallas_call(
        cut_kernel,
        grid=(1,),
        in_specs=[
            pl.BlockSpec(memory_space=pltpu.SMEM),
            pl.BlockSpec((PANEL, width), lambda i: (0, 0)),
        ],
        out_specs=pl.BlockSpec((chips, 2, depth, 2 * PANEL), lambda i: (0, 0, 0, 0)),
        out_shape=jax.ShapeDtypeStruct((chips, 2, depth, 2 * PANEL), jnp.float32),
        compiler_params=pltpu.CompilerParams(vmem_limit_bytes=60 * 2**20),
        name="cut_panel",
    )(place, factor_panels)


def invert_kernel(d_ref, x_ref):
    def dot(a, b):
        return jnp.dot(a, b, precision=HIGHEST, preferred_element_type=jnp.float32)

    base = 128
    row = lax.broadcasted_iota(jnp.int32, (base, base), 0)
    col = lax.broadcasted_iota(jnp.int32, (base, base), 1)
    spots = [
        (slice(n, n + base), slice(k * PANEL + n, k * PANEL + n + base))
        for k in range(PANELS)
        for n in range(0, PANEL, base)
    ]
    blocks = [d_ref[0, r, c] for r, c in spots]
    inverses = [jnp.where(row == col, 1.0 / jnp.where(row == col, b, 1.0), 0.0) for b in blocks]
    size = 1
    while size < base:
        joins = (row // (2 * size) == col // (2 * size)) & (row // size != col // size) & (row > col)
        inner = [dot(jnp.where(joins, b, 0.0), x) for b, x in zip(blocks, inverses)]
        inverses = [x - dot(x, y) for x, y in zip(inverses, inner)]
        size *= 2
    x_ref[...] = jnp.zeros_like(x_ref)
    for (r, c), x in zip(spots, inverses):
        x_ref[r, c] = x
    size = base
    while size < PANEL:
        for k in range(PANELS):
            for start in range(0, PANEL, 2 * size):
                top = slice(start, start + size)
                low = slice(start + size, start + 2 * size)
                left = slice(k * PANEL + start, k * PANEL + start + size)
                right = slice(k * PANEL + start + size, k * PANEL + start + 2 * size)
                x_ref[low, left] = -dot(x_ref[low, right], dot(d_ref[0, low, left], x_ref[top, left]))
        size *= 2


def invert_panels(panels):
    _, rows, width = panels.shape
    return pl.pallas_call(
        invert_kernel,
        grid=(1,),
        in_specs=[pl.BlockSpec((1, rows, width), lambda i: (0, 0, 0))],
        out_specs=pl.BlockSpec((rows, width), lambda i: (0, 0)),
        out_shape=jax.ShapeDtypeStruct((rows, width), jnp.float32),
        compiler_params=pltpu.CompilerParams(vmem_limit_bytes=40 * 2**20),
        cost_estimate=SMALL,
        name="invert_panels",
    )(panels)


def split(value):
    high = value.astype(jnp.bfloat16)
    return high, (value - high.astype(jnp.float32)).astype(jnp.bfloat16)


def one_hot(pairs, first, rows):
    pair = lax.broadcasted_iota(jnp.int32, (rows, pairs.shape[1]), 0) + first
    return jnp.where(pair == pairs, 1.0, 0.0).astype(jnp.bfloat16)


def place_kernel(place_ref, pairs_ref, received_ref, update_ref, out_ref, chosen_ref):
    part = pl.program_id(0)
    total, rank = out_ref.shape
    stride = received_ref.shape[0] // total
    lanes = rank // 128
    parts = stride // lanes

    @pl.when(part == 0)
    def _():
        chosen_ref[...] = one_hot(pairs_ref[...], 0, total)

    value = jnp.concatenate(
        [received_ref[pl.ds(h * parts + part, total, stride=stride), :] for h in range(lanes)], axis=1
    )
    own = (place_ref[1] == 1) & (part * rank < PANEL)
    high, low = split(jnp.where(own, 0.0, value))
    placed = jnp.dot(chosen_ref[...], high, preferred_element_type=jnp.float32)
    placed += jnp.dot(chosen_ref[...], low, preferred_element_type=jnp.float32)
    out_ref[...] = placed - update_ref[...]


def place_rows(place, slot_pair, received, update):
    total, width = update.shape
    rank = 256
    columns = pl.BlockSpec((total, rank), lambda i: (0, i))
    return pl.pallas_call(
        place_kernel,
        grid=(width // rank,),
        in_specs=[
            pl.BlockSpec(memory_space=pltpu.SMEM),
            pl.BlockSpec((1, total), lambda i: (0, 0)),
            pl.BlockSpec(received.shape, lambda i: (0, 0)),
            columns,
        ],
        out_specs=columns,
        out_shape=jax.ShapeDtypeStruct((total, width), jnp.float32),
        scratch_shapes=[pltpu.VMEM((total, total), jnp.bfloat16)],
        compiler_params=pltpu.CompilerParams(vmem_limit_bytes=48 * 2**20),
        name="place_rows",
    )(place, slot_pair, received, update)


def dot_split(a, b):
    def dot(x, y):
        return lax.dot_general(x, y, (((1,), (1,)), ((), ())), preferred_element_type=jnp.float32)

    return dot(a[0], b[0]) + (dot(a[0], b[1]) + dot(a[1], b[0]))


def arrange_kernel(place_ref, pairs_ref, *refs):
    pieces, (right_ref, panels_ref) = refs[:-2], refs[-2:]
    half = len(pieces) // 2
    inner_count = pieces[0].shape[0]
    rows = inner_count * 8
    core, pair, y, z = place_ref[2], place_ref[3], place_ref[4], place_ref[5]
    gradients = jnp.concatenate([ref[:, 16:, :].reshape(rows, PANEL) for ref in pieces], axis=0)
    chosen = one_hot(pairs_ref[...], 0, pairs_ref.shape[1])
    right = None
    for part in split(gradients):
        moved = jnp.dot(chosen, part, preferred_element_type=jnp.float32)
        right = moved if right is None else right + moved
    right_ref[...] = right
    for n, ref in enumerate(pieces):
        kind = core if n < half else 1 - core
        second, outer = n % half // 4, n % 4
        for inner in range(inner_count):
            y_back, z_back = (outer, inner) if second == 0 else (inner, outer)
            chip = lax.rem(y + 4 - y_back, 4) * 4 + lax.rem(z + 4 - z_back, 4)
            for j in range(2):
                unit = chip * 4 + lax.rem(pair + 4 - (2 * second + j), 4)
                place_rows_at = pl.ds(pl.multiple_of(unit * 8, 8), 8)
                panels_ref[kind, place_rows_at, :] = ref[inner, 8 * j : 8 * j + 8, :]


def arrange_rows(place, pairs, pieces):
    inner, depth, width = pieces[0].shape
    total = pairs.shape[1]
    return pl.pallas_call(
        arrange_kernel,
        grid=(width // PANEL,),
        in_specs=[
            pl.BlockSpec(memory_space=pltpu.SMEM),
            pl.BlockSpec(pairs.shape, lambda k: (0, 0)),
        ]
        + [pl.BlockSpec((inner, depth, PANEL), lambda k: (0, 0, k))] * len(pieces),
        out_specs=[
            pl.BlockSpec((total, PANEL), lambda k: (0, k)),
            pl.BlockSpec((2, PANEL, PANEL), lambda k: (0, 0, k)),
        ],
        out_shape=[
            jax.ShapeDtypeStruct((total, width), jnp.float32),
            jax.ShapeDtypeStruct((2, PANEL, width), jnp.float32),
        ],
        compiler_params=pltpu.CompilerParams(vmem_limit_bytes=60 * 2**20),
        cost_estimate=SMALL,
        name="arrange_rows",
    )(place, pairs, *pieces)


def split_kernel(value_ref, high_ref, low_ref):
    high_ref[...], low_ref[...] = split(value_ref[...])


def split_factor(factor_panels):
    rows, depth = factor_panels.shape
    block = pl.BlockSpec((256, depth), lambda i: (i, 0))
    return pl.pallas_call(
        split_kernel,
        grid=(rows // 256,),
        in_specs=[block],
        out_specs=[block, block],
        out_shape=[jax.ShapeDtypeStruct((rows, depth), jnp.bfloat16)] * 2,
        compiler_params=pltpu.CompilerParams(vmem_limit_bytes=60 * 2**20),
        cost_estimate=pl.CostEstimate(
            flops=3 * rows * depth, bytes_accessed=8 * rows * depth, transcendentals=0
        ),
        name="split_factor",
    )(factor_panels)


def solve_kernel(
    place_ref, right_ref, inverse_ref, panels_ref, factor_high_ref, factor_low_ref, out_ref,
    solved_ref, high_ref, low_ref,
):
    step = pl.program_id(0)
    width = out_ref.shape[1]

    @pl.when(step == 0)
    def _():

        def factor(ref, k):
            return split(ref[:, k * PANEL : (k + 1) * PANEL])

        for k in range(PANELS):
            columns = slice(k * PANEL, (k + 1) * PANEL)
            right = right_ref[:, columns]
            for j in range(k):
                before = slice(j * PANEL, (j + 1) * PANEL)
                solved = (high_ref[:, before], low_ref[:, before])
                right -= dot_split(solved, factor(panels_ref.at[0], k * (k - 1) // 2 + j))
            value = dot_split(split(right), factor(inverse_ref, k))
            solved_ref[k] = value
            high_ref[:, columns], low_ref[:, columns] = split(value)

    out_ref[...] = dot_split(
        (high_ref[...], low_ref[...]), (factor_high_ref[...], factor_low_ref[...])
    )

    for i in range(PANEL // width):

        @pl.when((place_ref[1] == 1) & (step == i))
        def _():
            out_ref[...] = -solved_ref[place_ref[0], :, i * width : (i + 1) * width]


def solve_and_update(place, right, inverse, panels, factor_parts):
    rows, depth = factor_parts[0].shape
    total = right.shape[0]
    width = 256
    whole = lambda v: pl.BlockSpec(v.shape, lambda i: (0, 0))
    block = pl.BlockSpec((width, depth), lambda i: (i, 0))
    return pl.pallas_call(
        solve_kernel,
        grid=(rows // width,),
        in_specs=[
            pl.BlockSpec(memory_space=pltpu.SMEM),
            whole(right),
            whole(inverse),
            pl.BlockSpec((1,) + panels.shape[1:], lambda i: (1, 0, 0)),
            block,
            block,
        ],
        out_specs=pl.BlockSpec((total, width), lambda i: (0, i)),
        out_shape=jax.ShapeDtypeStruct((total, rows), jnp.float32),
        scratch_shapes=[
            pltpu.VMEM((PANELS, total, PANEL), jnp.float32),
            pltpu.VMEM((total, depth), jnp.bfloat16),
            pltpu.VMEM((total, depth), jnp.bfloat16),
        ],
        compiler_params=pltpu.CompilerParams(vmem_limit_bytes=48 * 2**20),
        cost_estimate=SMALL,
        name="solve_and_update",
    )(place, right, inverse, panels, *factor_parts)


def along(value, axis, shift):
    if axis == "pair":
        return lax.ppermute(value, "pair", [(p, (p + shift) % 4) for p in range(4)])
    stride = 8 if axis == "y" else 2
    ring = lambda f: f - f // stride % 4 * stride + (f // stride + shift) % 4 * stride
    n_feat = lax.axis_size("feat")
    return lax.ppermute(value, "feat", [(f, ring(f)) for f in range(n_feat)])


def gather_panels(arrived, panel_part, send, factor_panels, feat, pair, slot_pair):
    slots, width = panel_part.shape
    first = jnp.concatenate([arrived[k, :, :PANEL] for k in range(3)], axis=1)
    second = jnp.concatenate([arrived[1, :, :PANEL], arrived[2]], axis=1)
    shard = jnp.where(feat % 2 == 0, first, second)
    depth = shard.shape[0]
    groups = panel_part.reshape(4, slots // 4, width)
    piece = lambda k: lax.dynamic_index_in_dim(groups, (pair + k) % 4, 0, keepdims=False)
    load = lambda k: jnp.concatenate([shard, piece(k)], axis=0)
    pieces = [load(0)] + [along(load(k), "pair", k) for k in range(1, 4)]
    halves = [
        jnp.concatenate([v[:depth] for v in two] + [v[depth:] for v in two], axis=0)[None]
        for two in (pieces[:2], pieces[2:])
    ]
    orders = (("z", "y"), ("y", "z"))
    ring = lambda part, axis: jnp.concatenate(
        [part] + [along(part, axis, k) for k in range(1, 4)], axis=0
    )
    halves = [ring(part, order[0]) for part, order in zip(halves, orders)]
    halves, factor_panels = lax.optimization_barrier((halves, factor_panels))
    parts = split_factor(factor_panels)
    a, b = [[along(part, order[1], k) for k in range(1, 4)] for part, order in zip(halves, orders)]
    a, b, send, parts = lax.optimization_barrier((a, b, send, parts))
    near = [halves[0]] + a + [halves[1]] + b
    cores = [(f, f ^ 1) for f in range(lax.axis_size("feat"))]
    pieces = near + [lax.ppermute(piece, "feat", cores) for piece in near]
    n = lax.broadcasted_iota(jnp.int32, (128, 128), 0)
    other_core, second, outer, inner, back = n // 64, n // 32 % 2, n // 8 % 4, n // 2 % 4, n % 2
    y_back = jnp.where(second == 0, outer, inner)
    z_back = jnp.where(second == 0, inner, outer)
    y = (feat // 8 + 4 - y_back) % 4
    z = (feat // 2 % 4 + 4 - z_back) % 4
    core = (feat % 2 + other_core) % 2
    x = (pair + 4 - (2 * second + back)) % 4
    source = ((y * 4 + z) * 2 + core) * 4 + x
    chosen = (source == lax.broadcasted_iota(jnp.int32, (128, 128), 1)).astype(jnp.float32)
    table = slot_pair.reshape(128, slots // 4).astype(jnp.float32)
    pairs = jnp.dot(chosen, table, precision=HIGHEST, preferred_element_type=jnp.float32)
    pairs = jnp.round(pairs).astype(jnp.int32).reshape(1, 32 * slots)
    return pieces, pairs, send, parts


def per_device(in_factors, out_factors, token_counts, slot_pair, factor_panels):
    slots, _, _, rank = in_factors.shape
    n_pair = lax.axis_size("pair")
    n_feat = lax.axis_size("feat")
    per_group = slots // n_pair
    feat = lax.axis_index("feat")
    pair = lax.axis_index("pair")
    total = n_feat * slots

    place = jnp.stack(
        [jnp.minimum(feat, PANELS - 1), (feat < PANELS).astype(jnp.int32), feat % 2, pair]
        + [feat // 8, feat // 2 % 4]
    ).astype(jnp.int32)
    outgoing = cut_panel(place, factor_panels, n_feat, n_pair)
    arrived = lax.all_to_all(
        outgoing.reshape((n_feat,) + outgoing.shape[2:]), "feat", split_axis=0, concat_axis=0, tiled=True
    )
    send, panel_part = slot_gradients(token_counts, out_factors, in_factors, n_feat, n_pair)
    arrived, panel_part = lax.optimization_barrier((arrived, panel_part))
    pieces, pairs, send, parts = gather_panels(
        arrived, panel_part, send, factor_panels, feat, pair, slot_pair
    )
    received = lax.all_to_all(
        send.reshape((n_feat * n_pair,) + send.shape[2:]),
        ("feat", "pair"),
        split_axis=0,
        concat_axis=0,
        tiled=True,
    ).reshape(total * (rank // 128) * (rank // n_feat), 128)
    right, panels = arrange_rows(place, pairs, pieces)
    inverse = invert_panels(panels)
    update = solve_and_update(place, right, inverse, panels, parts)
    return place_rows(place, slot_pair, received, update)


def solution(mesh):
    return jax.shard_map(
        per_device,
        mesh=mesh,
        in_specs=(
            P(("feat", "pair"), None, None, None),
            P(("feat", "pair"), None, None, None),
            P(("feat", "pair"), None),
            P("pair", None),
            P("feat", None),
        ),
        out_specs=P("pair", "feat"),
        check_vma=False,
    )
```

```python
import jax
import jax.numpy as jnp
from jax import lax
from jax.experimental import pallas as pl
from jax.experimental.pallas import tpu as pltpu
from jax.sharding import PartitionSpec as P

PANEL = 512
PANELS = 3
HIGHEST = lax.Precision.HIGHEST
SMALL = pl.CostEstimate(flops=1, bytes_accessed=1, transcendentals=0)


def gradient_kernel(counts_ref, out_ref, in_ref, send_ref, panel_ref):
    slot = pl.program_id(0)
    depth, rank = out_ref.shape[2:]
    position = lax.broadcasted_iota(jnp.int32, (depth, 128), 0)
    total = None
    for side in range(2):
        kept = jnp.where(position < counts_ref[slot, side], 1.0, 0.0).astype(jnp.bfloat16)
        weights = jnp.concatenate([kept] * (rank // 128), axis=1)
        product = lax.dot_general(
            out_ref[0, side] * weights,
            in_ref[0, side],
            (((0,), (0,)), ((), ())),
            preferred_element_type=jnp.float32,
        )
        total = product if side == 0 else total - product
    feats, _, _, lanes, parts, lane = send_ref.shape
    for h in range(lanes):
        columns = total[:, h * lane : (h + 1) * lane]
        send_ref[:, 0, 0, h] = columns.reshape(feats, parts, lane)
    for k in range(PANELS):
        for i in range(PANEL // rank):
            columns = slice(k * PANEL + i * rank, k * PANEL + (i + 1) * rank)
            panel_ref[pl.ds(slot, 1), columns] = total[8 * k + i : 8 * k + i + 1, :]


def slot_gradients(token_counts, out_factors, in_factors, n_feat, n_pair):
    slots, sides, depth, rank = in_factors.shape
    per_group = slots // n_pair
    factors = pl.BlockSpec((1, sides, depth, rank), lambda k, counts: (k, 0, 0, 0))
    return pl.pallas_call(
        gradient_kernel,
        grid_spec=pltpu.PrefetchScalarGridSpec(
            num_scalar_prefetch=1,
            grid=(slots,),
            in_specs=[factors, factors],
            out_specs=[
                pl.BlockSpec(
                    (n_feat, 1, 1, rank // 128, rank // n_feat, 128),
                    lambda k, counts: (0, k // per_group, k % per_group, 0, 0, 0),
                ),
                pl.BlockSpec((slots, PANELS * PANEL), lambda k, counts: (0, 0)),
            ],
        ),
        out_shape=[
            jax.ShapeDtypeStruct(
                (n_feat, n_pair, per_group, rank // 128, rank // n_feat, 128), jnp.float32
            ),
            jax.ShapeDtypeStruct((slots, PANELS * PANEL), jnp.float32),
        ],
        compiler_params=pltpu.CompilerParams(vmem_limit_bytes=60 * 2**20),
        cost_estimate=pl.CostEstimate(
            flops=2 * slots * sides * depth * rank * rank, bytes_accessed=24 * 2**20, transcendentals=0
        ),
        name="slot_gradients",
    )(token_counts, out_factors, in_factors)


def cut_kernel(place_ref, panel_ref, send_ref):
    chips, _, depth, _ = send_ref.shape
    groups = PANEL // (chips * depth)
    for chip in range(chips):
        rows = pl.ds(pl.multiple_of((chip * groups + place_ref[3]) * depth, depth), depth)
        diagonal = panel_ref[rows, (PANELS - 1) * PANEL :]
        for k in range(PANELS - 1):
            diagonal = jnp.where(
                place_ref[0] == k, panel_ref[rows, k * PANEL : (k + 1) * PANEL], diagonal
            )
        send_ref[chip, 0, :, :PANEL] = diagonal
        send_ref[chip, 0, :, PANEL:] = jnp.zeros((depth, PANEL), jnp.float32)
        send_ref[chip, 1] = panel_ref[rows, : 2 * PANEL]


def cut_panel(place, factor_panels, n_feat, n_pair):
    width = factor_panels.shape[1]
    chips = n_feat // 2
    depth = PANEL // (chips * n_pair)
    return pl.pallas_call(
        cut_kernel,
        grid=(1,),
        in_specs=[
            pl.BlockSpec(memory_space=pltpu.SMEM),
            pl.BlockSpec((PANEL, width), lambda i: (0, 0)),
        ],
        out_specs=pl.BlockSpec((chips, 2, depth, 2 * PANEL), lambda i: (0, 0, 0, 0)),
        out_shape=jax.ShapeDtypeStruct((chips, 2, depth, 2 * PANEL), jnp.float32),
        compiler_params=pltpu.CompilerParams(vmem_limit_bytes=60 * 2**20),
        name="cut_panel",
    )(place, factor_panels)


def invert_kernel(d_ref, x_ref):
    def dot(a, b):
        return jnp.dot(a, b, precision=HIGHEST, preferred_element_type=jnp.float32)

    base = 128
    row = lax.broadcasted_iota(jnp.int32, (base, base), 0)
    col = lax.broadcasted_iota(jnp.int32, (base, base), 1)
    spots = [
        (slice(n, n + base), slice(k * PANEL + n, k * PANEL + n + base))
        for k in range(PANELS)
        for n in range(0, PANEL, base)
    ]
    blocks = [d_ref[0, r, c] for r, c in spots]
    inverses = [jnp.where(row == col, 1.0 / jnp.where(row == col, b, 1.0), 0.0) for b in blocks]
    size = 1
    while size < base:
        joins = (row // (2 * size) == col // (2 * size)) & (row // size != col // size) & (row > col)
        inner = [dot(jnp.where(joins, b, 0.0), x) for b, x in zip(blocks, inverses)]
        inverses = [x - dot(x, y) for x, y in zip(inverses, inner)]
        size *= 2
    x_ref[...] = jnp.zeros_like(x_ref)
    for (r, c), x in zip(spots, inverses):
        x_ref[r, c] = x
    size = base
    while size < PANEL:
        for k in range(PANELS):
            for start in range(0, PANEL, 2 * size):
                top = slice(start, start + size)
                low = slice(start + size, start + 2 * size)
                left = slice(k * PANEL + start, k * PANEL + start + size)
                right = slice(k * PANEL + start + size, k * PANEL + start + 2 * size)
                x_ref[low, left] = -dot(x_ref[low, right], dot(d_ref[0, low, left], x_ref[top, left]))
        size *= 2


def split(value):
    high = value.astype(jnp.bfloat16)
    return high, (value - high.astype(jnp.float32)).astype(jnp.bfloat16)


def one_hot(pairs, first, rows):
    pair = lax.broadcasted_iota(jnp.int32, (rows, pairs.shape[1]), 0) + first
    return jnp.where(pair == pairs, 1.0, 0.0).astype(jnp.bfloat16)


def place_kernel(place_ref, pairs_ref, received_ref, update_ref, out_ref, high_ref, low_ref):
    step = pl.program_id(0)
    rows = out_ref.shape[0]
    parts, total, rank = high_ref.shape

    @pl.when(step == 0)
    def _():
        for i in range(parts):
            lanes = rank // 128
            value = jnp.concatenate(
                [
                    received_ref[pl.ds(h * parts + i, total, stride=lanes * parts), :]
                    for h in range(lanes)
                ],
                axis=1,
            )
            if i * rank < PANEL:
                value = jnp.where(place_ref[1] == 1, 0.0, value)
            high_ref[i], low_ref[i] = split(value)

    chosen = one_hot(pairs_ref[...], step * rows, rows)
    for i in range(parts):
        placed = jnp.dot(chosen, high_ref[i], preferred_element_type=jnp.float32)
        placed += jnp.dot(chosen, low_ref[i], preferred_element_type=jnp.float32)
        columns = slice(i * rank, (i + 1) * rank)
        out_ref[:, columns] = placed - update_ref[:, columns]


def place_rows(place, slot_pair, received, update):
    total, width = update.shape
    rank = 2 * received.shape[1]
    parts = width // rank
    rows = 128
    return pl.pallas_call(
        place_kernel,
        grid=(total // rows,),
        in_specs=[
            pl.BlockSpec(memory_space=pltpu.SMEM),
            pl.BlockSpec((1, total), lambda i: (0, 0)),
            pl.BlockSpec(received.shape, lambda i: (0, 0)),
            pl.BlockSpec((rows, width), lambda i: (i, 0)),
        ],
        out_specs=pl.BlockSpec((rows, width), lambda i: (i, 0)),
        out_shape=jax.ShapeDtypeStruct((total, width), jnp.float32),
        scratch_shapes=[
            pltpu.VMEM((parts, total, rank), jnp.bfloat16),
            pltpu.VMEM((parts, total, rank), jnp.bfloat16),
        ],
        compiler_params=pltpu.CompilerParams(vmem_limit_bytes=48 * 2**20),
        name="place_rows",
    )(place, slot_pair, received, update)


def dot_split(a, b):
    def dot(x, y):
        return lax.dot_general(x, y, (((1,), (1,)), ((), ())), preferred_element_type=jnp.float32)

    return dot(a[0], b[0]) + (dot(a[0], b[1]) + dot(a[1], b[0]))


def arrange_kernel(place_ref, pairs_ref, *refs):
    pieces, (right_ref, panels_ref) = refs[:-2], refs[-2:]
    half = len(pieces) // 2
    inner_count = pieces[0].shape[0]
    rows = inner_count * 8
    core, pair, y, z = place_ref[2], place_ref[3], place_ref[4], place_ref[5]
    gradients = jnp.concatenate([ref[:, 16:, :].reshape(rows, PANEL) for ref in pieces], axis=0)
    chosen = one_hot(pairs_ref[...], 0, pairs_ref.shape[1])
    right = None
    for part in split(gradients):
        moved = jnp.dot(chosen, part, preferred_element_type=jnp.float32)
        right = moved if right is None else right + moved
    right_ref[...] = right
    for n, ref in enumerate(pieces):
        kind = core if n < half else 1 - core
        second, outer = n % half // 4, n % 4
        for inner in range(inner_count):
            y_back, z_back = (outer, inner) if second == 0 else (inner, outer)
            chip = lax.rem(y + 4 - y_back, 4) * 4 + lax.rem(z + 4 - z_back, 4)
            for j in range(2):
                unit = chip * 4 + lax.rem(pair + 4 - (2 * second + j), 4)
                place_rows_at = pl.ds(pl.multiple_of(unit * 8, 8), 8)
                panels_ref[kind, place_rows_at, :] = ref[inner, 8 * j : 8 * j + 8, :]


def arrange_rows(place, pairs, pieces):
    inner, depth, width = pieces[0].shape
    total = pairs.shape[1]
    return pl.pallas_call(
        arrange_kernel,
        grid=(width // PANEL,),
        in_specs=[
            pl.BlockSpec(memory_space=pltpu.SMEM),
            pl.BlockSpec(pairs.shape, lambda k: (0, 0)),
        ]
        + [pl.BlockSpec((inner, depth, PANEL), lambda k: (0, 0, k))] * len(pieces),
        out_specs=[
            pl.BlockSpec((total, PANEL), lambda k: (0, k)),
            pl.BlockSpec((2, PANEL, PANEL), lambda k: (0, 0, k)),
        ],
        out_shape=[
            jax.ShapeDtypeStruct((total, width), jnp.float32),
            jax.ShapeDtypeStruct((2, PANEL, width), jnp.float32),
        ],
        compiler_params=pltpu.CompilerParams(vmem_limit_bytes=60 * 2**20),
        cost_estimate=SMALL,
        name="arrange_rows",
    )(place, pairs, *pieces)


def solve_kernel(
    place_ref, right_ref, panels_ref, factor_ref, out_ref,
    inverse_ref, solved_ref, high_ref, low_ref,
):
    step = pl.program_id(0)
    width = out_ref.shape[1]

    @pl.when(step == 0)
    def _():
        invert_kernel(panels_ref, inverse_ref)

        def factor(ref, k):
            return split(ref[:, k * PANEL : (k + 1) * PANEL])

        for k in range(PANELS):
            columns = slice(k * PANEL, (k + 1) * PANEL)
            right = right_ref[:, columns]
            for j in range(k):
                before = slice(j * PANEL, (j + 1) * PANEL)
                solved = (high_ref[:, before], low_ref[:, before])
                right -= dot_split(solved, factor(panels_ref.at[1], k * (k - 1) // 2 + j))
            value = dot_split(split(right), factor(inverse_ref, k))
            solved_ref[k] = value
            high_ref[:, columns], low_ref[:, columns] = split(value)

    out_ref[...] = dot_split((high_ref[...], low_ref[...]), split(factor_ref[...]))

    for i in range(PANEL // width):

        @pl.when((place_ref[1] == 1) & (step == i))
        def _():
            out_ref[...] = -solved_ref[place_ref[0], :, i * width : (i + 1) * width]


def solve_and_update(place, right, panels, factor_panels):
    rows, depth = factor_panels.shape
    total = right.shape[0]
    width = 256
    whole = lambda v: pl.BlockSpec(v.shape, lambda i: (0, 0))
    block = pl.BlockSpec((width, depth), lambda i: (i, 0))
    return pl.pallas_call(
        solve_kernel,
        grid=(rows // width,),
        in_specs=[
            pl.BlockSpec(memory_space=pltpu.SMEM),
            whole(right),
            pl.BlockSpec(panels.shape, lambda i: (0, 0, 0)),
            block,
        ],
        out_specs=pl.BlockSpec((total, width), lambda i: (0, i)),
        out_shape=jax.ShapeDtypeStruct((total, rows), jnp.float32),
        scratch_shapes=[
            pltpu.VMEM(panels.shape[1:], jnp.float32),
            pltpu.VMEM((PANELS, total, PANEL), jnp.float32),
            pltpu.VMEM((total, depth), jnp.bfloat16),
            pltpu.VMEM((total, depth), jnp.bfloat16),
        ],
        compiler_params=pltpu.CompilerParams(vmem_limit_bytes=56 * 2**20),
        cost_estimate=SMALL,
        name="solve_and_update",
    )(place, right, panels, factor_panels)


def along(value, axis, shift):
    if axis == "pair":
        return lax.ppermute(value, "pair", [(p, (p + shift) % 4) for p in range(4)])
    stride = 8 if axis == "y" else 2
    ring = lambda f: f - f // stride % 4 * stride + (f // stride + shift) % 4 * stride
    n_feat = lax.axis_size("feat")
    return lax.ppermute(value, "feat", [(f, ring(f)) for f in range(n_feat)])


def gather_panels(arrived, panel_part, send, feat, pair, slot_pair):
    slots, width = panel_part.shape
    first = jnp.concatenate([arrived[k, :, :PANEL] for k in range(3)], axis=1)
    second = jnp.concatenate([arrived[1, :, :PANEL], arrived[2]], axis=1)
    shard = jnp.where(feat % 2 == 0, first, second)
    depth = shard.shape[0]
    groups = panel_part.reshape(4, slots // 4, width)
    piece = lambda k: lax.dynamic_index_in_dim(groups, (pair + k) % 4, 0, keepdims=False)
    load = lambda k: jnp.concatenate([shard, piece(k)], axis=0)
    pieces = [load(0)] + [along(load(k), "pair", k) for k in range(1, 4)]
    halves = [
        jnp.concatenate([v[:depth] for v in two] + [v[depth:] for v in two], axis=0)[None]
        for two in (pieces[:2], pieces[2:])
    ]
    orders = (("z", "y"), ("y", "z"))
    ring = lambda part, axis: jnp.concatenate(
        [part] + [along(part, axis, k) for k in range(1, 4)], axis=0
    )
    halves = [ring(part, order[0]) for part, order in zip(halves, orders)]
    halves, slot_pair = lax.optimization_barrier((halves, slot_pair))
    n = lax.broadcasted_iota(jnp.int32, (128, 128), 0)
    other_core, second, outer, inner, back = n // 64, n // 32 % 2, n // 8 % 4, n // 2 % 4, n % 2
    y_back = jnp.where(second == 0, outer, inner)
    z_back = jnp.where(second == 0, inner, outer)
    y = (feat // 8 + 4 - y_back) % 4
    z = (feat // 2 % 4 + 4 - z_back) % 4
    core = (feat % 2 + other_core) % 2
    x = (pair + 4 - (2 * second + back)) % 4
    source = ((y * 4 + z) * 2 + core) * 4 + x
    chosen = (source == lax.broadcasted_iota(jnp.int32, (128, 128), 1)).astype(jnp.float32)
    table = slot_pair.reshape(128, slots // 4).astype(jnp.float32)
    pairs = jnp.dot(chosen, table, precision=HIGHEST, preferred_element_type=jnp.float32)
    pairs = jnp.round(pairs).astype(jnp.int32).reshape(1, 32 * slots)
    a, b = [[along(part, order[1], k) for k in range(1, 4)] for part, order in zip(halves, orders)]
    a, b, send, pairs = lax.optimization_barrier((a, b, send, pairs))
    near = [halves[0]] + a + [halves[1]] + b
    cores = [(f, f ^ 1) for f in range(lax.axis_size("feat"))]
    pieces = near + [lax.ppermute(piece, "feat", cores) for piece in near]
    return pieces, pairs, send


def per_device(in_factors, out_factors, token_counts, slot_pair, factor_panels):
    slots, _, _, rank = in_factors.shape
    n_pair = lax.axis_size("pair")
    n_feat = lax.axis_size("feat")
    per_group = slots // n_pair
    feat = lax.axis_index("feat")
    pair = lax.axis_index("pair")
    total = n_feat * slots

    place = jnp.stack(
        [jnp.minimum(feat, PANELS - 1), (feat < PANELS).astype(jnp.int32), feat % 2, pair]
        + [feat // 8, feat // 2 % 4]
    ).astype(jnp.int32)
    outgoing = cut_panel(place, factor_panels, n_feat, n_pair)
    arrived = lax.all_to_all(
        outgoing.reshape((n_feat,) + outgoing.shape[2:]), "feat", split_axis=0, concat_axis=0, tiled=True
    )
    send, panel_part = slot_gradients(token_counts, out_factors, in_factors, n_feat, n_pair)
    arrived, panel_part = lax.optimization_barrier((arrived, panel_part))
    pieces, pairs, send = gather_panels(arrived, panel_part, send, feat, pair, slot_pair)
    received = lax.all_to_all(
        send.reshape((n_feat * n_pair,) + send.shape[2:]),
        ("feat", "pair"),
        split_axis=0,
        concat_axis=0,
        tiled=True,
    ).reshape(total * (rank // 128) * (rank // n_feat), 128)
    right, panels = arrange_rows(place, pairs, pieces)
    update = solve_and_update(place, right, panels, factor_panels)
    return place_rows(place, slot_pair, received, update)


def solution(mesh):
    return jax.shard_map(
        per_device,
        mesh=mesh,
        in_specs=(
            P(("feat", "pair"), None, None, None),
            P(("feat", "pair"), None, None, None),
            P(("feat", "pair"), None),
            P("pair", None),
            P("feat", None),
        ),
        out_specs=P("pair", "feat"),
        check_vma=False,
    )
```

```python
import jax
import jax.numpy as jnp
from jax import lax
from jax.experimental import pallas as pl
from jax.experimental.pallas import tpu as pltpu
from jax.sharding import PartitionSpec as P

PANEL = 512
PANELS = 3
HIGHEST = lax.Precision.HIGHEST
SMALL = pl.CostEstimate(flops=1, bytes_accessed=1, transcendentals=0)


def gradient_kernel(counts_ref, out_ref, in_ref, send_ref, panel_ref):
    slot = pl.program_id(0)
    depth, rank = out_ref.shape[2:]
    position = lax.broadcasted_iota(jnp.int32, (depth, 128), 0)
    total = None
    for side in range(2):
        kept = jnp.where(position < counts_ref[slot, side], 1.0, 0.0).astype(jnp.bfloat16)
        weights = jnp.concatenate([kept] * (rank // 128), axis=1)
        product = lax.dot_general(
            out_ref[0, side] * weights,
            in_ref[0, side],
            (((0,), (0,)), ((), ())),
            preferred_element_type=jnp.float32,
        )
        total = product if side == 0 else total - product
    feats, _, _, lanes, parts, lane = send_ref.shape
    for h in range(lanes):
        columns = total[:, h * lane : (h + 1) * lane]
        send_ref[:, 0, 0, h] = columns.reshape(feats, parts, lane)
    for k in range(PANELS):
        for i in range(PANEL // rank):
            columns = slice(k * PANEL + i * rank, k * PANEL + (i + 1) * rank)
            panel_ref[pl.ds(slot, 1), columns] = total[8 * k + i : 8 * k + i + 1, :]


def slot_gradients(token_counts, out_factors, in_factors, n_feat, n_pair):
    slots, sides, depth, rank = in_factors.shape
    per_group = slots // n_pair
    factors = pl.BlockSpec((1, sides, depth, rank), lambda k, counts: (k, 0, 0, 0))
    return pl.pallas_call(
        gradient_kernel,
        grid_spec=pltpu.PrefetchScalarGridSpec(
            num_scalar_prefetch=1,
            grid=(slots,),
            in_specs=[factors, factors],
            out_specs=[
                pl.BlockSpec(
                    (n_feat, 1, 1, rank // 128, rank // n_feat, 128),
                    lambda k, counts: (0, k // per_group, k % per_group, 0, 0, 0),
                ),
                pl.BlockSpec((slots, PANELS * PANEL), lambda k, counts: (0, 0)),
            ],
        ),
        out_shape=[
            jax.ShapeDtypeStruct(
                (n_feat, n_pair, per_group, rank // 128, rank // n_feat, 128), jnp.float32
            ),
            jax.ShapeDtypeStruct((slots, PANELS * PANEL), jnp.float32),
        ],
        compiler_params=pltpu.CompilerParams(vmem_limit_bytes=60 * 2**20),
        cost_estimate=pl.CostEstimate(
            flops=2 * slots * sides * depth * rank * rank, bytes_accessed=24 * 2**20, transcendentals=0
        ),
        name="slot_gradients",
    )(token_counts, out_factors, in_factors)


def cut_kernel(place_ref, panel_ref, send_ref):
    chips, _, depth, _ = send_ref.shape
    groups = PANEL // (chips * depth)
    for chip in range(chips):
        rows = pl.ds(pl.multiple_of((chip * groups + place_ref[3]) * depth, depth), depth)
        diagonal = panel_ref[rows, (PANELS - 1) * PANEL :]
        for k in range(PANELS - 1):
            diagonal = jnp.where(
                place_ref[0] == k, panel_ref[rows, k * PANEL : (k + 1) * PANEL], diagonal
            )
        send_ref[chip, 0, :, :PANEL] = diagonal
        send_ref[chip, 0, :, PANEL:] = jnp.zeros((depth, PANEL), jnp.float32)
        send_ref[chip, 1] = panel_ref[rows, : 2 * PANEL]


def cut_panel(place, factor_panels, n_feat, n_pair):
    width = factor_panels.shape[1]
    chips = n_feat // 2
    depth = PANEL // (chips * n_pair)
    return pl.pallas_call(
        cut_kernel,
        grid=(1,),
        in_specs=[
            pl.BlockSpec(memory_space=pltpu.SMEM),
            pl.BlockSpec((PANEL, width), lambda i: (0, 0)),
        ],
        out_specs=pl.BlockSpec((chips, 2, depth, 2 * PANEL), lambda i: (0, 0, 0, 0)),
        out_shape=jax.ShapeDtypeStruct((chips, 2, depth, 2 * PANEL), jnp.float32),
        compiler_params=pltpu.CompilerParams(vmem_limit_bytes=60 * 2**20),
        name="cut_panel",
    )(place, factor_panels)


def invert_kernel(d_ref, x_ref):
    def dot(a, b):
        (a, a_low), (b, b_low) = split(a), split(b)
        product = lambda x, y: jnp.dot(x, y, preferred_element_type=jnp.float32)
        return product(a, b) + (product(a, b_low) + product(a_low, b))

    base = 128
    row = lax.broadcasted_iota(jnp.int32, (base, base), 0)
    col = lax.broadcasted_iota(jnp.int32, (base, base), 1)
    spots = [
        (slice(n, n + base), slice(k * PANEL + n, k * PANEL + n + base))
        for k in range(PANELS)
        for n in range(0, PANEL, base)
    ]
    blocks = [d_ref[0, r, c] for r, c in spots]
    inverses = [jnp.where(row == col, 1.0 / jnp.where(row == col, b, 1.0), 0.0) for b in blocks]
    size = 1
    while size < base:
        joins = (row // (2 * size) == col // (2 * size)) & (row // size != col // size) & (row > col)
        inner = [dot(jnp.where(joins, b, 0.0), x) for b, x in zip(blocks, inverses)]
        inverses = [x - dot(x, y) for x, y in zip(inverses, inner)]
        size *= 2
    x_ref[...] = jnp.zeros_like(x_ref)
    for (r, c), x in zip(spots, inverses):
        x_ref[r, c] = x
    size = base
    while size < PANEL:
        for k in range(PANELS):
            for start in range(0, PANEL, 2 * size):
                top = slice(start, start + size)
                low = slice(start + size, start + 2 * size)
                left = slice(k * PANEL + start, k * PANEL + start + size)
                right = slice(k * PANEL + start + size, k * PANEL + start + 2 * size)
                x_ref[low, left] = -dot(x_ref[low, right], dot(d_ref[0, low, left], x_ref[top, left]))
        size *= 2


def split(value):
    high = value.astype(jnp.bfloat16)
    return high, (value - high.astype(jnp.float32)).astype(jnp.bfloat16)


def one_hot(pairs, first, rows):
    pair = lax.broadcasted_iota(jnp.int32, (rows, pairs.shape[1]), 0) + first
    return jnp.where(pair == pairs, 1.0, 0.0).astype(jnp.bfloat16)


def place_kernel(place_ref, pairs_ref, received_ref, update_ref, out_ref, high_ref, low_ref):
    step = pl.program_id(0)
    rows = out_ref.shape[0]
    parts, total, rank = high_ref.shape

    @pl.when(step == 0)
    def _():
        for i in range(parts):
            lanes = rank // 128
            value = jnp.concatenate(
                [
                    received_ref[pl.ds(h * parts + i, total, stride=lanes * parts), :]
                    for h in range(lanes)
                ],
                axis=1,
            )
            if i * rank < PANEL:
                value = jnp.where(place_ref[1] == 1, 0.0, value)
            high_ref[i], low_ref[i] = split(value)

    chosen = one_hot(pairs_ref[...], step * rows, rows)
    for i in range(parts):
        placed = jnp.dot(chosen, high_ref[i], preferred_element_type=jnp.float32)
        placed += jnp.dot(chosen, low_ref[i], preferred_element_type=jnp.float32)
        columns = slice(i * rank, (i + 1) * rank)
        out_ref[:, columns] = placed - update_ref[:, columns]


def place_rows(place, slot_pair, received, update):
    total, width = update.shape
    rank = 2 * received.shape[1]
    parts = width // rank
    rows = 128
    return pl.pallas_call(
        place_kernel,
        grid=(total // rows,),
        in_specs=[
            pl.BlockSpec(memory_space=pltpu.SMEM),
            pl.BlockSpec((1, total), lambda i: (0, 0)),
            pl.BlockSpec(received.shape, lambda i: (0, 0)),
            pl.BlockSpec((rows, width), lambda i: (i, 0)),
        ],
        out_specs=pl.BlockSpec((rows, width), lambda i: (i, 0)),
        out_shape=jax.ShapeDtypeStruct((total, width), jnp.float32),
        scratch_shapes=[
            pltpu.VMEM((parts, total, rank), jnp.bfloat16),
            pltpu.VMEM((parts, total, rank), jnp.bfloat16),
        ],
        compiler_params=pltpu.CompilerParams(vmem_limit_bytes=48 * 2**20),
        name="place_rows",
    )(place, slot_pair, received, update)


def dot_split(a, b):
    def dot(x, y):
        return lax.dot_general(x, y, (((1,), (1,)), ((), ())), preferred_element_type=jnp.float32)

    return dot(a[0], b[0]) + (dot(a[0], b[1]) + dot(a[1], b[0]))


def arrange_kernel(place_ref, pairs_ref, *refs):
    pieces, (right_ref, panels_ref) = refs[:-2], refs[-2:]
    half = len(pieces) // 2
    inner_count = pieces[0].shape[0]
    rows = inner_count * 8
    core, pair, y, z = place_ref[2], place_ref[3], place_ref[4], place_ref[5]
    gradients = jnp.concatenate([ref[:, 16:, :].reshape(rows, PANEL) for ref in pieces], axis=0)
    chosen = one_hot(pairs_ref[...], 0, pairs_ref.shape[1])
    right = None
    for part in split(gradients):
        moved = jnp.dot(chosen, part, preferred_element_type=jnp.float32)
        right = moved if right is None else right + moved
    right_ref[...] = right
    for n, ref in enumerate(pieces):
        kind = core if n < half else 1 - core
        second, outer = n % half // 4, n % 4
        for inner in range(inner_count):
            y_back, z_back = (outer, inner) if second == 0 else (inner, outer)
            chip = lax.rem(y + 4 - y_back, 4) * 4 + lax.rem(z + 4 - z_back, 4)
            for j in range(2):
                unit = chip * 4 + lax.rem(pair + 4 - (2 * second + j), 4)
                place_rows_at = pl.ds(pl.multiple_of(unit * 8, 8), 8)
                panels_ref[kind, place_rows_at, :] = ref[inner, 8 * j : 8 * j + 8, :]


def arrange_rows(place, pairs, pieces):
    inner, depth, width = pieces[0].shape
    total = pairs.shape[1]
    return pl.pallas_call(
        arrange_kernel,
        grid=(width // PANEL,),
        in_specs=[
            pl.BlockSpec(memory_space=pltpu.SMEM),
            pl.BlockSpec(pairs.shape, lambda k: (0, 0)),
        ]
        + [pl.BlockSpec((inner, depth, PANEL), lambda k: (0, 0, k))] * len(pieces),
        out_specs=[
            pl.BlockSpec((total, PANEL), lambda k: (0, k)),
            pl.BlockSpec((2, PANEL, PANEL), lambda k: (0, 0, k)),
        ],
        out_shape=[
            jax.ShapeDtypeStruct((total, width), jnp.float32),
            jax.ShapeDtypeStruct((2, PANEL, width), jnp.float32),
        ],
        compiler_params=pltpu.CompilerParams(vmem_limit_bytes=60 * 2**20),
        cost_estimate=SMALL,
        name="arrange_rows",
    )(place, pairs, *pieces)


def solve_kernel(
    place_ref, right_ref, panels_ref, factor_ref, out_ref,
    inverse_ref, solved_ref, high_ref, low_ref,
):
    step = pl.program_id(0)
    width = out_ref.shape[1]

    @pl.when(step == 0)
    def _():
        invert_kernel(panels_ref, inverse_ref)

        def factor(ref, k):
            return split(ref[:, k * PANEL : (k + 1) * PANEL])

        for k in range(PANELS):
            columns = slice(k * PANEL, (k + 1) * PANEL)
            right = right_ref[:, columns]
            for j in range(k):
                before = slice(j * PANEL, (j + 1) * PANEL)
                solved = (high_ref[:, before], low_ref[:, before])
                right -= dot_split(solved, factor(panels_ref.at[1], k * (k - 1) // 2 + j))
            value = dot_split(split(right), factor(inverse_ref, k))
            solved_ref[k] = value
            high_ref[:, columns], low_ref[:, columns] = split(value)

    out_ref[...] = dot_split((high_ref[...], low_ref[...]), split(factor_ref[...]))

    for i in range(PANEL // width):

        @pl.when((place_ref[1] == 1) & (step == i))
        def _():
            out_ref[...] = -solved_ref[place_ref[0], :, i * width : (i + 1) * width]


def solve_and_update(place, right, panels, factor_panels):
    rows, depth = factor_panels.shape
    total = right.shape[0]
    width = 256
    whole = lambda v: pl.BlockSpec(v.shape, lambda i: (0, 0))
    block = pl.BlockSpec((width, depth), lambda i: (i, 0))
    return pl.pallas_call(
        solve_kernel,
        grid=(rows // width,),
        in_specs=[
            pl.BlockSpec(memory_space=pltpu.SMEM),
            whole(right),
            pl.BlockSpec(panels.shape, lambda i: (0, 0, 0)),
            block,
        ],
        out_specs=pl.BlockSpec((total, width), lambda i: (0, i)),
        out_shape=jax.ShapeDtypeStruct((total, rows), jnp.float32),
        scratch_shapes=[
            pltpu.VMEM(panels.shape[1:], jnp.float32),
            pltpu.VMEM((PANELS, total, PANEL), jnp.float32),
            pltpu.VMEM((total, depth), jnp.bfloat16),
            pltpu.VMEM((total, depth), jnp.bfloat16),
        ],
        compiler_params=pltpu.CompilerParams(vmem_limit_bytes=56 * 2**20),
        cost_estimate=SMALL,
        name="solve_and_update",
    )(place, right, panels, factor_panels)


def along(value, axis, shift):
    if axis == "pair":
        return lax.ppermute(value, "pair", [(p, (p + shift) % 4) for p in range(4)])
    stride = 8 if axis == "y" else 2
    ring = lambda f: f - f // stride % 4 * stride + (f // stride + shift) % 4 * stride
    n_feat = lax.axis_size("feat")
    return lax.ppermute(value, "feat", [(f, ring(f)) for f in range(n_feat)])


def gather_panels(arrived, panel_part, send, feat, pair, slot_pair):
    slots, width = panel_part.shape
    first = jnp.concatenate([arrived[k, :, :PANEL] for k in range(3)], axis=1)
    second = jnp.concatenate([arrived[1, :, :PANEL], arrived[2]], axis=1)
    shard = jnp.where(feat % 2 == 0, first, second)
    depth = shard.shape[0]
    groups = panel_part.reshape(4, slots // 4, width)
    piece = lambda k: lax.dynamic_index_in_dim(groups, (pair + k) % 4, 0, keepdims=False)
    load = lambda k: jnp.concatenate([shard, piece(k)], axis=0)
    pieces = [load(0)] + [along(load(k), "pair", k) for k in range(1, 4)]
    halves = [
        jnp.concatenate([v[:depth] for v in two] + [v[depth:] for v in two], axis=0)[None]
        for two in (pieces[:2], pieces[2:])
    ]
    orders = (("z", "y"), ("y", "z"))
    ring = lambda part, axis: jnp.concatenate(
        [part] + [along(part, axis, k) for k in range(1, 4)], axis=0
    )
    halves = [ring(part, order[0]) for part, order in zip(halves, orders)]
    halves, slot_pair = lax.optimization_barrier((halves, slot_pair))
    n = lax.broadcasted_iota(jnp.int32, (128, 128), 0)
    other_core, second, outer, inner, back = n // 64, n // 32 % 2, n // 8 % 4, n // 2 % 4, n % 2
    y_back = jnp.where(second == 0, outer, inner)
    z_back = jnp.where(second == 0, inner, outer)
    y = (feat // 8 + 4 - y_back) % 4
    z = (feat // 2 % 4 + 4 - z_back) % 4
    core = (feat % 2 + other_core) % 2
    x = (pair + 4 - (2 * second + back)) % 4
    source = ((y * 4 + z) * 2 + core) * 4 + x
    chosen = (source == lax.broadcasted_iota(jnp.int32, (128, 128), 1)).astype(jnp.float32)
    table = slot_pair.reshape(128, slots // 4).astype(jnp.float32)
    pairs = jnp.dot(chosen, table, precision=HIGHEST, preferred_element_type=jnp.float32)
    pairs = jnp.round(pairs).astype(jnp.int32).reshape(1, 32 * slots)
    a, b = [[along(part, order[1], k) for k in range(1, 4)] for part, order in zip(halves, orders)]
    a, b, send, pairs = lax.optimization_barrier((a, b, send, pairs))
    near = [halves[0]] + a + [halves[1]] + b
    cores = [(f, f ^ 1) for f in range(lax.axis_size("feat"))]
    pieces = near + [lax.ppermute(piece, "feat", cores) for piece in near]
    return pieces, pairs, send


def per_device(in_factors, out_factors, token_counts, slot_pair, factor_panels):
    slots, _, _, rank = in_factors.shape
    n_pair = lax.axis_size("pair")
    n_feat = lax.axis_size("feat")
    per_group = slots // n_pair
    feat = lax.axis_index("feat")
    pair = lax.axis_index("pair")
    total = n_feat * slots

    place = jnp.stack(
        [jnp.minimum(feat, PANELS - 1), (feat < PANELS).astype(jnp.int32), feat % 2, pair]
        + [feat // 8, feat // 2 % 4]
    ).astype(jnp.int32)
    outgoing = cut_panel(place, factor_panels, n_feat, n_pair)
    arrived = lax.all_to_all(
        outgoing.reshape((n_feat,) + outgoing.shape[2:]), "feat", split_axis=0, concat_axis=0, tiled=True
    )
    send, panel_part = slot_gradients(token_counts, out_factors, in_factors, n_feat, n_pair)
    arrived, panel_part = lax.optimization_barrier((arrived, panel_part))
    pieces, pairs, send = gather_panels(arrived, panel_part, send, feat, pair, slot_pair)
    received = lax.all_to_all(
        send.reshape((n_feat * n_pair,) + send.shape[2:]),
        ("feat", "pair"),
        split_axis=0,
        concat_axis=0,
        tiled=True,
    ).reshape(total * (rank // 128) * (rank // n_feat), 128)
    right, panels = arrange_rows(place, pairs, pieces)
    update = solve_and_update(place, right, panels, factor_panels)
    return place_rows(place, slot_pair, received, update)


def solution(mesh):
    return jax.shard_map(
        per_device,
        mesh=mesh,
        in_specs=(
            P(("feat", "pair"), None, None, None),
            P(("feat", "pair"), None, None, None),
            P(("feat", "pair"), None),
            P("pair", None),
            P("feat", None),
        ),
        out_specs=P("pair", "feat"),
        check_vma=False,
    )
```

```python
import jax
import jax.numpy as jnp
from jax import lax
from jax.experimental import pallas as pl
from jax.experimental.pallas import tpu as pltpu
from jax.sharding import PartitionSpec as P

PANEL = 512
PANELS = 3
HIGHEST = lax.Precision.HIGHEST
SMALL = pl.CostEstimate(flops=1, bytes_accessed=1, transcendentals=0)


def gradient_kernel(counts_ref, out_ref, in_ref, send_ref, panel_ref):
    slot = pl.program_id(0)
    depth, rank = out_ref.shape[2:]
    position = lax.broadcasted_iota(jnp.int32, (depth, 128), 0)
    total = None
    for side in range(2):
        kept = jnp.where(position < counts_ref[slot, side], 1.0, 0.0).astype(jnp.bfloat16)
        weights = jnp.concatenate([kept] * (rank // 128), axis=1)
        product = lax.dot_general(
            out_ref[0, side] * weights,
            in_ref[0, side],
            (((0,), (0,)), ((), ())),
            preferred_element_type=jnp.float32,
        )
        total = product if side == 0 else total - product
    feats, _, _, lanes, parts, lane = send_ref.shape
    for h in range(lanes):
        columns = total[:, h * lane : (h + 1) * lane]
        send_ref[:, 0, 0, h] = columns.reshape(feats, parts, lane)
    for k in range(PANELS):
        for i in range(PANEL // rank):
            columns = slice(k * PANEL + i * rank, k * PANEL + (i + 1) * rank)
            panel_ref[pl.ds(slot, 1), columns] = total[8 * k + i : 8 * k + i + 1, :]


def slot_gradients(token_counts, out_factors, in_factors, n_feat, n_pair):
    slots, sides, depth, rank = in_factors.shape
    per_group = slots // n_pair
    factors = pl.BlockSpec((1, sides, depth, rank), lambda k, counts: (k, 0, 0, 0))
    return pl.pallas_call(
        gradient_kernel,
        grid_spec=pltpu.PrefetchScalarGridSpec(
            num_scalar_prefetch=1,
            grid=(slots,),
            in_specs=[factors, factors],
            out_specs=[
                pl.BlockSpec(
                    (n_feat, 1, 1, rank // 128, rank // n_feat, 128),
                    lambda k, counts: (0, k // per_group, k % per_group, 0, 0, 0),
                ),
                pl.BlockSpec((slots, PANELS * PANEL), lambda k, counts: (0, 0)),
            ],
        ),
        out_shape=[
            jax.ShapeDtypeStruct(
                (n_feat, n_pair, per_group, rank // 128, rank // n_feat, 128), jnp.float32
            ),
            jax.ShapeDtypeStruct((slots, PANELS * PANEL), jnp.float32),
        ],
        compiler_params=pltpu.CompilerParams(vmem_limit_bytes=60 * 2**20),
        cost_estimate=pl.CostEstimate(
            flops=2 * slots * sides * depth * rank * rank, bytes_accessed=24 * 2**20, transcendentals=0
        ),
        name="slot_gradients",
    )(token_counts, out_factors, in_factors)


def cut_kernel(place_ref, panel_ref, send_ref):
    chips, _, depth, _ = send_ref.shape
    groups = PANEL // (chips * depth)
    for chip in range(chips):
        rows = pl.ds(pl.multiple_of((chip * groups + place_ref[3]) * depth, depth), depth)
        diagonal = panel_ref[rows, (PANELS - 1) * PANEL :]
        for k in range(PANELS - 1):
            diagonal = jnp.where(
                place_ref[0] == k, panel_ref[rows, k * PANEL : (k + 1) * PANEL], diagonal
            )
        send_ref[chip, 0, :, :PANEL] = diagonal
        send_ref[chip, 0, :, PANEL:] = jnp.zeros((depth, PANEL), jnp.float32)
        send_ref[chip, 1] = panel_ref[rows, : 2 * PANEL]


def cut_panel(place, factor_panels, n_feat, n_pair):
    width = factor_panels.shape[1]
    chips = n_feat // 2
    depth = PANEL // (chips * n_pair)
    return pl.pallas_call(
        cut_kernel,
        grid=(1,),
        in_specs=[
            pl.BlockSpec(memory_space=pltpu.SMEM),
            pl.BlockSpec((PANEL, width), lambda i: (0, 0)),
        ],
        out_specs=pl.BlockSpec((chips, 2, depth, 2 * PANEL), lambda i: (0, 0, 0, 0)),
        out_shape=jax.ShapeDtypeStruct((chips, 2, depth, 2 * PANEL), jnp.float32),
        compiler_params=pltpu.CompilerParams(vmem_limit_bytes=60 * 2**20),
        name="cut_panel",
    )(place, factor_panels)


def invert_kernel(d_ref, x_ref):
    def dot(a, b):
        (a, a_low), (b, b_low) = split(a), split(b)
        product = lambda x, y: jnp.dot(x, y, preferred_element_type=jnp.float32)
        return product(a, b) + (product(a, b_low) + product(a_low, b))

    base = 128
    row = lax.broadcasted_iota(jnp.int32, (base, base), 0)
    col = lax.broadcasted_iota(jnp.int32, (base, base), 1)
    spots = [
        (slice(n, n + base), slice(k * PANEL + n, k * PANEL + n + base))
        for k in range(PANELS)
        for n in range(0, PANEL, base)
    ]
    blocks = [d_ref[0, r, c] for r, c in spots]
    inverses = [jnp.where(row == col, 1.0 / jnp.where(row == col, b, 1.0), 0.0) for b in blocks]
    size = 1
    while size < base:
        joins = (row // (2 * size) == col // (2 * size)) & (row // size != col // size) & (row > col)
        inner = [dot(jnp.where(joins, b, 0.0), x) for b, x in zip(blocks, inverses)]
        inverses = [x - dot(x, y) for x, y in zip(inverses, inner)]
        size *= 2
    x_ref[...] = jnp.zeros_like(x_ref)
    for (r, c), x in zip(spots, inverses):
        x_ref[r, c] = x
    size = base
    while size < PANEL:
        for k in range(PANELS):
            for start in range(0, PANEL, 2 * size):
                top = slice(start, start + size)
                low = slice(start + size, start + 2 * size)
                left = slice(k * PANEL + start, k * PANEL + start + size)
                right = slice(k * PANEL + start + size, k * PANEL + start + 2 * size)
                x_ref[low, left] = -dot(x_ref[low, right], dot(d_ref[0, low, left], x_ref[top, left]))
        size *= 2


def split(value):
    high = value.astype(jnp.bfloat16)
    return high, (value - high.astype(jnp.float32)).astype(jnp.bfloat16)


def one_hot(pairs, first, rows):
    pair = lax.broadcasted_iota(jnp.int32, (rows, pairs.shape[1]), 0) + first
    return jnp.where(pair == pairs, 1.0, 0.0).astype(jnp.bfloat16)


def place_kernel(place_ref, pairs_ref, received_ref, update_ref, out_ref, high_ref, low_ref):
    step = pl.program_id(0)
    rows = out_ref.shape[0]
    parts, total, rank = high_ref.shape

    @pl.when(step == 0)
    def _():
        lanes = rank // 128
        tiles = received_ref[...].reshape(total // 8, 8, lanes, parts, 128)
        for h in range(lanes):
            turned = jnp.swapaxes(tiles[:, :, h], 1, 2)
            columns = slice(h * 128, (h + 1) * 128)
            for i in range(parts):
                value = turned[:, i].reshape(total, 128)
                if i * rank < PANEL:
                    value = jnp.where(place_ref[1] == 1, 0.0, value)
                high_ref[i, :, columns], low_ref[i, :, columns] = split(value)

    chosen = one_hot(pairs_ref[...], step * rows, rows)
    for i in range(parts):
        placed = jnp.dot(chosen, high_ref[i], preferred_element_type=jnp.float32)
        placed += jnp.dot(chosen, low_ref[i], preferred_element_type=jnp.float32)
        columns = slice(i * rank, (i + 1) * rank)
        out_ref[:, columns] = placed - update_ref[:, columns]


def place_rows(place, slot_pair, received, update):
    total, width = update.shape
    rank = 2 * received.shape[1]
    parts = width // rank
    rows = 128
    return pl.pallas_call(
        place_kernel,
        grid=(total // rows,),
        in_specs=[
            pl.BlockSpec(memory_space=pltpu.SMEM),
            pl.BlockSpec((1, total), lambda i: (0, 0)),
            pl.BlockSpec(received.shape, lambda i: (0, 0)),
            pl.BlockSpec((rows, width), lambda i: (i, 0)),
        ],
        out_specs=pl.BlockSpec((rows, width), lambda i: (i, 0)),
        out_shape=jax.ShapeDtypeStruct((total, width), jnp.float32),
        scratch_shapes=[
            pltpu.VMEM((parts, total, rank), jnp.bfloat16),
            pltpu.VMEM((parts, total, rank), jnp.bfloat16),
        ],
        compiler_params=pltpu.CompilerParams(vmem_limit_bytes=48 * 2**20),
        name="place_rows",
    )(place, slot_pair, received, update)


def dot_split(a, b):
    def dot(x, y):
        return lax.dot_general(x, y, (((1,), (1,)), ((), ())), preferred_element_type=jnp.float32)

    return dot(a[0], b[0]) + (dot(a[0], b[1]) + dot(a[1], b[0]))


def arrange_kernel(place_ref, pairs_ref, *refs):
    pieces, (right_ref, panels_ref) = refs[:-2], refs[-2:]
    half = len(pieces) // 2
    inner_count = pieces[0].shape[0]
    rows = inner_count * 8
    core, pair, y, z = place_ref[2], place_ref[3], place_ref[4], place_ref[5]
    gradients = jnp.concatenate([ref[:, 16:, :].reshape(rows, PANEL) for ref in pieces], axis=0)
    chosen = one_hot(pairs_ref[...], 0, pairs_ref.shape[1])
    right = None
    for part in split(gradients):
        moved = jnp.dot(chosen, part, preferred_element_type=jnp.float32)
        right = moved if right is None else right + moved
    right_ref[...] = right
    for n, ref in enumerate(pieces):
        kind = core if n < half else 1 - core
        second, outer = n % half // 4, n % 4
        for inner in range(inner_count):
            y_back, z_back = (outer, inner) if second == 0 else (inner, outer)
            chip = lax.rem(y + 4 - y_back, 4) * 4 + lax.rem(z + 4 - z_back, 4)
            for j in range(2):
                unit = chip * 4 + lax.rem(pair + 4 - (2 * second + j), 4)
                place_rows_at = pl.ds(pl.multiple_of(unit * 8, 8), 8)
                panels_ref[kind, place_rows_at, :] = ref[inner, 8 * j : 8 * j + 8, :]


def arrange_rows(place, pairs, pieces):
    inner, depth, width = pieces[0].shape
    total = pairs.shape[1]
    return pl.pallas_call(
        arrange_kernel,
        grid=(width // PANEL,),
        in_specs=[
            pl.BlockSpec(memory_space=pltpu.SMEM),
            pl.BlockSpec(pairs.shape, lambda k: (0, 0)),
        ]
        + [pl.BlockSpec((inner, depth, PANEL), lambda k: (0, 0, k))] * len(pieces),
        out_specs=[
            pl.BlockSpec((total, PANEL), lambda k: (0, k)),
            pl.BlockSpec((2, PANEL, PANEL), lambda k: (0, 0, k)),
        ],
        out_shape=[
            jax.ShapeDtypeStruct((total, width), jnp.float32),
            jax.ShapeDtypeStruct((2, PANEL, width), jnp.float32),
        ],
        compiler_params=pltpu.CompilerParams(vmem_limit_bytes=60 * 2**20),
        cost_estimate=SMALL,
        name="arrange_rows",
    )(place, pairs, *pieces)


def solve_kernel(
    place_ref, right_ref, panels_ref, factor_ref, out_ref,
    inverse_ref, solved_ref, high_ref, low_ref,
):
    step = pl.program_id(0)
    width = out_ref.shape[1]

    @pl.when(step == 0)
    def _():
        invert_kernel(panels_ref, inverse_ref)

        def factor(ref, k):
            return split(ref[:, k * PANEL : (k + 1) * PANEL])

        for k in range(PANELS):
            columns = slice(k * PANEL, (k + 1) * PANEL)
            right = right_ref[:, columns]
            for j in range(k):
                before = slice(j * PANEL, (j + 1) * PANEL)
                solved = (high_ref[:, before], low_ref[:, before])
                right -= dot_split(solved, factor(panels_ref.at[1], k * (k - 1) // 2 + j))
            value = dot_split(split(right), factor(inverse_ref, k))
            solved_ref[k] = value
            high_ref[:, columns], low_ref[:, columns] = split(value)

    out_ref[...] = dot_split((high_ref[...], low_ref[...]), split(factor_ref[...]))

    for i in range(PANEL // width):

        @pl.when((place_ref[1] == 1) & (step == i))
        def _():
            out_ref[...] = -solved_ref[place_ref[0], :, i * width : (i + 1) * width]


def solve_and_update(place, right, panels, factor_panels):
    rows, depth = factor_panels.shape
    total = right.shape[0]
    width = 256
    whole = lambda v: pl.BlockSpec(v.shape, lambda i: (0, 0))
    block = pl.BlockSpec((width, depth), lambda i: (i, 0))
    return pl.pallas_call(
        solve_kernel,
        grid=(rows // width,),
        in_specs=[
            pl.BlockSpec(memory_space=pltpu.SMEM),
            whole(right),
            pl.BlockSpec(panels.shape, lambda i: (0, 0, 0)),
            block,
        ],
        out_specs=pl.BlockSpec((total, width), lambda i: (0, i)),
        out_shape=jax.ShapeDtypeStruct((total, rows), jnp.float32),
        scratch_shapes=[
            pltpu.VMEM(panels.shape[1:], jnp.float32),
            pltpu.VMEM((PANELS, total, PANEL), jnp.float32),
            pltpu.VMEM((total, depth), jnp.bfloat16),
            pltpu.VMEM((total, depth), jnp.bfloat16),
        ],
        compiler_params=pltpu.CompilerParams(vmem_limit_bytes=56 * 2**20),
        cost_estimate=SMALL,
        name="solve_and_update",
    )(place, right, panels, factor_panels)


def along(value, axis, shift):
    if axis == "pair":
        return lax.ppermute(value, "pair", [(p, (p + shift) % 4) for p in range(4)])
    stride = 8 if axis == "y" else 2
    ring = lambda f: f - f // stride % 4 * stride + (f // stride + shift) % 4 * stride
    n_feat = lax.axis_size("feat")
    return lax.ppermute(value, "feat", [(f, ring(f)) for f in range(n_feat)])


def gather_panels(arrived, panel_part, send, feat, pair, slot_pair):
    slots, width = panel_part.shape
    first = jnp.concatenate([arrived[k, :, :PANEL] for k in range(3)], axis=1)
    second = jnp.concatenate([arrived[1, :, :PANEL], arrived[2]], axis=1)
    shard = jnp.where(feat % 2 == 0, first, second)
    depth = shard.shape[0]
    groups = panel_part.reshape(4, slots // 4, width)
    piece = lambda k: lax.dynamic_index_in_dim(groups, (pair + k) % 4, 0, keepdims=False)
    load = lambda k: jnp.concatenate([shard, piece(k)], axis=0)
    pieces = [load(0)] + [along(load(k), "pair", k) for k in range(1, 4)]
    halves = [
        jnp.concatenate([v[:depth] for v in two] + [v[depth:] for v in two], axis=0)[None]
        for two in (pieces[:2], pieces[2:])
    ]
    orders = (("z", "y"), ("y", "z"))
    ring = lambda part, axis: jnp.concatenate(
        [part] + [along(part, axis, k) for k in range(1, 4)], axis=0
    )
    halves = [ring(part, order[0]) for part, order in zip(halves, orders)]
    halves, slot_pair = lax.optimization_barrier((halves, slot_pair))
    n = lax.broadcasted_iota(jnp.int32, (128, 128), 0)
    other_core, second, outer, inner, back = n // 64, n // 32 % 2, n // 8 % 4, n // 2 % 4, n % 2
    y_back = jnp.where(second == 0, outer, inner)
    z_back = jnp.where(second == 0, inner, outer)
    y = (feat // 8 + 4 - y_back) % 4
    z = (feat // 2 % 4 + 4 - z_back) % 4
    core = (feat % 2 + other_core) % 2
    x = (pair + 4 - (2 * second + back)) % 4
    source = ((y * 4 + z) * 2 + core) * 4 + x
    chosen = (source == lax.broadcasted_iota(jnp.int32, (128, 128), 1)).astype(jnp.float32)
    table = slot_pair.reshape(128, slots // 4).astype(jnp.float32)
    pairs = jnp.dot(chosen, table, precision=HIGHEST, preferred_element_type=jnp.float32)
    pairs = jnp.round(pairs).astype(jnp.int32).reshape(1, 32 * slots)
    a, b = [[along(part, order[1], k) for k in range(1, 4)] for part, order in zip(halves, orders)]
    a, b, send, pairs = lax.optimization_barrier((a, b, send, pairs))
    near = [halves[0]] + a + [halves[1]] + b
    cores = [(f, f ^ 1) for f in range(lax.axis_size("feat"))]
    pieces = near + [lax.ppermute(piece, "feat", cores) for piece in near]
    return pieces, pairs, send


def per_device(in_factors, out_factors, token_counts, slot_pair, factor_panels):
    slots, _, _, rank = in_factors.shape
    n_pair = lax.axis_size("pair")
    n_feat = lax.axis_size("feat")
    per_group = slots // n_pair
    feat = lax.axis_index("feat")
    pair = lax.axis_index("pair")
    total = n_feat * slots

    place = jnp.stack(
        [jnp.minimum(feat, PANELS - 1), (feat < PANELS).astype(jnp.int32), feat % 2, pair]
        + [feat // 8, feat // 2 % 4]
    ).astype(jnp.int32)
    outgoing = cut_panel(place, factor_panels, n_feat, n_pair)
    arrived = lax.all_to_all(
        outgoing.reshape((n_feat,) + outgoing.shape[2:]), "feat", split_axis=0, concat_axis=0, tiled=True
    )
    send, panel_part = slot_gradients(token_counts, out_factors, in_factors, n_feat, n_pair)
    arrived, panel_part = lax.optimization_barrier((arrived, panel_part))
    pieces, pairs, send = gather_panels(arrived, panel_part, send, feat, pair, slot_pair)
    received = lax.all_to_all(
        send.reshape((n_feat * n_pair,) + send.shape[2:]),
        ("feat", "pair"),
        split_axis=0,
        concat_axis=0,
        tiled=True,
    ).reshape(total * (rank // 128) * (rank // n_feat), 128)
    right, panels = arrange_rows(place, pairs, pieces)
    update = solve_and_update(place, right, panels, factor_panels)
    return place_rows(place, slot_pair, received, update)


def solution(mesh):
    return jax.shard_map(
        per_device,
        mesh=mesh,
        in_specs=(
            P(("feat", "pair"), None, None, None),
            P(("feat", "pair"), None, None, None),
            P(("feat", "pair"), None),
            P("pair", None),
            P("feat", None),
        ),
        out_specs=P("pair", "feat"),
        check_vma=False,
    )
```
